256 devices in a mesh: snapshot: 4 (over z_lo), face: 32 (over y, x, core), row: 2 (over z_hi).
Axes of the slice: x: 4, y: 4, z: 8 (z_hi: 2, z_lo: 4; z = z_hi * 4 + z_lo), core: 2. Of those that a mesh axis runs over, the one named last changes fastest.
Arguments:
- surface_field: bfloat16 [32, 48, 48, 2048], P('face', 'row', None, 'snapshot'), may hold values from -12 to 12, as said below
- ocean_mask: int32 [32, 48, 48], P('face', 'row'), may hold values from 0 to 1, as said below
- cell_area: float32 [32, 48, 48], P('face', 'row'), may hold values from 0.25 to 4
- tile_links: int32 [32, 2], replicated, may hold values from 0 to 31
- edge_turns: int32 [32, 2], replicated, may hold values from 0 to 3
Outputs:
- anomaly: bfloat16 [32, 48, 48, 2048], P('face', 'row', None, 'snapshot')
- gram_matrix: float32 [2048, 2048], P(('snapshot', 'face', 'row'))
The draws below stay inside these ranges and needn't reach their ends.
Inputs may be any that keep to these rules, and one draw needn't show every extreme that they name: `surface_field`: temporally correlated over a few snapshots, independent from cell to cell. `ocean_mask`: within the first 24 rows of all tiles together exactly half the cells are ocean, and likewise within the last 24 rows; land fractions differ strongly from tile to tile, and some tile is ocean in full.
All inputs are finite; a program needn't handle non-finite values.
Results may differ from the reference program's by a relative error of at most 0.001.
Values may be sent and summed in bfloat16 or wider, within the bound.
A program may use at most 64 MiB of HBM per device.

```python
import math
import jax
import jax.numpy as jnp
from jax import lax

SNAPS = 2048
TILE_SIDE = 48
TILES = 32


def draw_surface_field(key, part):
    taps = 8
    decay = 0.8
    norm_total = sum((decay ** (2 * k) for k in range(taps))) ** 0.5
    key_noise, key_scale = jax.random.split(key)
    shape = (TILES, TILE_SIDE, TILE_SIDE, SNAPS + taps - 1)
    noise = jnp.clip(jax.random.normal(key_noise, shape, jnp.float32), -4.0, 4.0)
    result = jnp.zeros((TILES, TILE_SIDE, TILE_SIDE, SNAPS), jnp.float32)
    for k in range(taps):
        result = result + decay ** k / norm_total * noise[..., k:k + SNAPS]
    return result.astype(jnp.bfloat16)


def draw_ocean_mask(key, part):
    key_prio, key_pick, key_noise = jax.random.split(key, 3)
    half_rows = TILE_SIDE // 2
    priority = jax.random.randint(key_prio, (TILES,), 0, 8)
    picked = jax.random.randint(key_pick, (), 0, TILES)
    priority = jnp.where(jnp.arange(TILES) == picked, 8, priority)
    noise = jax.random.randint(key_noise, (2, TILES, half_rows, TILE_SIDE), 0, 4096)
    score = priority[None, :, None, None] * 4096 + noise
    flat_score = score.reshape(2, -1)
    order = jnp.argsort(-flat_score, axis=1, stable=True)
    ranks = jnp.argsort(order, axis=1, stable=True)
    total = TILES * half_rows * TILE_SIDE
    ocean = (ranks < total // 2).astype(jnp.int32).reshape(2, TILES, half_rows, TILE_SIDE)
    return jnp.transpose(ocean, (1, 0, 2, 3)).reshape(TILES, TILE_SIDE, TILE_SIDE)


def set_ends(values, rng, low, high):
    index_at = [jax.random.randint(jax.random.fold_in(rng, axis), (), 0, length) for axis, length in enumerate(values.shape)]
    longest = values.shape.index(max(values.shape))
    beside = index_at[:longest] + [(index_at[longest] + 1) % values.shape[longest]] + index_at[longest + 1:]
    return values.at[tuple(index_at)].set(low).at[tuple(beside)].set(high)


def shard_levels(stream_key, extent, shards, low, top_value):
    level, own = 1.0, jax.random.fold_in(stream_key, 6)
    for dim, parts in shards:
        heights = jnp.exp(jax.random.uniform(jax.random.fold_in(own, dim), (parts,), jnp.float32, low / len(shards), top_value / len(shards)))
        level = level * jnp.repeat(heights, extent[dim] // parts).reshape([-1 if axis == dim else 1 for axis in range(len(extent))])
    return level


def setup_inputs(seed: int = 0) -> dict:
    key_list = jax.random.split(jax.random.key(seed), 6)
    return {
        "surface_field": draw_surface_field(jax.random.fold_in(key_list[5], 71), 0),
        "ocean_mask": draw_ocean_mask(jax.random.fold_in(key_list[5], 71), 0),
        "cell_area": jnp.clip(jnp.exp(math.log(4.0) - 2.7725887 * jax.random.uniform(key_list[2], (TILES, TILE_SIDE, TILE_SIDE), jnp.float32) ** shard_levels(key_list[2], (TILES, TILE_SIDE, TILE_SIDE), ((0, 32), (1, 2)), -0.2, 0.2)), 0.25, 4.0),
        "tile_links": set_ends(jax.random.randint(key_list[3], (TILES, 2), 0, TILES), jax.random.fold_in(key_list[3], 1), 0, TILES - 1).astype(jnp.int32),
        "edge_turns": set_ends(jax.random.randint(key_list[4], (TILES, 2), 0, 4), jax.random.fold_in(key_list[4], 1), 0, 3).astype(jnp.int32),
    }


def edge_lines(surface_field, tile_links, edge_turns, side_index):
    linked = tile_links[:, side_index]
    west_line = surface_field[linked, :, 0, :]
    south_line = surface_field[linked, 0, :, :]
    turn_code = edge_turns[:, side_index][:, None, None]
    chosen_line = jnp.where(turn_code < 2, west_line, south_line)
    return jnp.where(turn_code % 2 == 1, chosen_line[:, ::-1], chosen_line)

def reference(surface_field, ocean_mask, cell_area, tile_links, edge_turns):
    east_lines = edge_lines(surface_field, tile_links, edge_turns, 0)
    north_lines = edge_lines(surface_field, tile_links, edge_turns, 1)

    def one_tile(gram_carry, inputs):
        tile_values, east_line, north_line, mask_tile, area_tile = inputs
        cell_values = tile_values.astype(jnp.float32)
        wider = jnp.concatenate([cell_values, east_line[:, None, :].astype(jnp.float32)], axis=1)
        grad_cols = wider[:, 1:] - wider[:, :-1]
        taller = jnp.concatenate([cell_values, north_line[None].astype(jnp.float32)], axis=0)
        grad_rows = taller[1:] - taller[:-1]
        slope_norm = jnp.sqrt(1.0 + (grad_cols * grad_cols + grad_rows * grad_rows) / area_tile[:, :, None])
        column_mean = lax.optimization_barrier(jnp.sum(slope_norm, axis=-1)) / SNAPS
        weighting = jnp.sqrt(area_tile) * mask_tile.astype(jnp.float32)
        anomaly_tile = (weighting[:, :, None] * (slope_norm - column_mean[:, :, None])).astype(jnp.bfloat16)
        flat_rows = anomaly_tile.reshape(-1, SNAPS).astype(jnp.float32)
        gram_carry = gram_carry + jnp.dot(flat_rows.T, flat_rows, precision=lax.Precision.HIGHEST)
        return (gram_carry, anomaly_tile)
    start_gram = jnp.zeros((SNAPS, SNAPS), jnp.float32)
    gram_total, anomaly = lax.scan(one_tile, start_gram, (surface_field, east_lines, north_lines, ocean_mask, cell_area))
    gram_matrix = gram_total * (1.0 / (TILES * TILE_SIDE * TILE_SIDE))
    return (anomaly, gram_matrix)
```

```python
import functools

import jax
import jax.numpy as jnp
from jax import lax
from jax.experimental import pallas as pl
from jax.experimental.pallas import tpu as pltpu
from jax.sharding import PartitionSpec as P

MESH = pl.DeviceIdType.MESH
BF16 = jnp.bfloat16
F32 = jnp.float32
SNAPS = 2048
ROWS = 24
SIDE = 48
BLK = 512
LANE = 128
GRAM_SCALE = 1.0 / (32 * 48 * 48)


def face_of(y, x, c):
    return (y * 4 + x) * 2 + c


def copy_to(src, dst, send_sem, recv_sem, device):
    return pltpu.make_async_remote_copy(
        src_ref=src,
        dst_ref=dst,
        send_sem=send_sem,
        recv_sem=recv_sem,
        device_id=device,
        device_id_type=MESH,
    )


def wait_bytes(ref, sem):
    pltpu.make_async_copy(ref, ref, sem).wait()


def kernel(
    links,
    turns,
    field,
    mask,
    area,
    anom,
    gram,
    tmp,
    lines,
    first,
    inner,
    gathered,
    chosen,
    arrived,
    east,
    north,
    slope,
    sums,
    own,
    end_in,
    mid_in,
    far_in,
    keep,
    give,
    take,
    mixed_d,
    mixed_t,
    red_d,
    red_t,
    piece_d,
    piece_t,
    fin_d,
    fin_t,
    halo_s,
    halo_r,
    sum_s,
    sum_r,
    str_s,
    end_r,
    mid_r,
    far_r,
    pair_s,
    pair_r,
    dir_s,
    dir_r,
    tra_s,
    tra_r,
    fin_s,
    fin_r,
):
    s = lax.axis_index("snapshot")
    f = lax.axis_index("face")
    r = lax.axis_index("row")
    chip = f // 2
    c = f % 2
    y = chip // 4
    x = chip % 4
    side = s // 2
    is_mid = (s == 1) | (s == 2)
    my_mid = 1 + side
    my_end = 3 * side
    other_mid = 2 - side
    other_end = 3 - 3 * side
    hfar = side
    hnear = 1 - side

    barrier = pltpu.get_barrier_semaphore()

    def greet(device):
        pl.semaphore_signal(barrier, inc=1, device_id=device, device_id_type=MESH)

    greet((s, f, 1 - r))
    greet((s, face_of(y, x, 1 - c), r))

    def greet_chip(step, carry):
        greet((s, 2 * ((chip + step) % 16) + c, r))
        return carry

    lax.fori_loop(1, 16, greet_chip, 0)

    def greet_plane(step, carry):
        greet(((s + step) % 4, f, r))
        greet(((s + step) % 4, f, 1 - r))
        return carry

    lax.fori_loop(1, 4, greet_plane, 0)
    pl.semaphore_wait(barrier, 23)

    tmp[...] = jnp.zeros_like(tmp)
    for i in range(ROWS):
        tmp[i : i + 1, :] = field[0, i, 0:16, :].astype(F32)[0:1]
    lines[r] = tmp[...].astype(BF16)
    row0 = field[0, 0].astype(F32)
    zpad = jnp.zeros((8, BLK), F32)
    for h in range(2):
        first[h] = jnp.concatenate([row0[24 * h : 24 * h + 24], zpad], axis=0).astype(BF16)

    @pl.when(r == 0)
    def _():
        lines[2:4] = first[...]
        a = copy_to(lines.at[0], lines.at[0], halo_s.at[0], halo_r.at[0], (s, f, 1))
        b = copy_to(first, lines.at[2:4], halo_s.at[1], halo_r.at[1], (s, f, 1))
        a.start()
        b.start()
        copy_to(lines.at[1], lines.at[1], halo_s.at[0], halo_r.at[0], (s, f, 1)).wait_recv()
        copy_to(first, inner, halo_s.at[1], halo_r.at[1], (s, f, 1)).wait_recv()
        a.wait_send()
        b.wait_send()

    @pl.when(r == 1)
    def _():
        inner[...] = first[...]
        a = copy_to(lines.at[1], lines.at[1], halo_s.at[0], halo_r.at[0], (s, f, 0))
        b = copy_to(first, inner, halo_s.at[1], halo_r.at[1], (s, f, 0))
        a.start()
        b.start()
        copy_to(lines.at[0], lines.at[0], halo_s.at[0], halo_r.at[0], (s, f, 0)).wait_recv()
        copy_to(first, lines.at[2:4], halo_s.at[1], halo_r.at[1], (s, f, 0)).wait_recv()
        a.wait_send()
        b.wait_send()

    gathered[c, y] = lines[...]
    ysends = []
    for step in range(1, 4):
        yd = (y + step) % 4
        d = copy_to(
            lines, gathered.at[c, y], halo_s.at[1 + step], halo_r.at[1 + step], (s, face_of(yd, x, c), r)
        )
        d.start()
        ysends.append(d)
    for step in range(1, 4):
        ysrc = (y + 4 - step) % 4
        copy_to(
            lines, gathered.at[c, ysrc], halo_s.at[1 + step], halo_r.at[1 + step], (s, f, r)
        ).wait_recv()
    d = copy_to(gathered.at[c], gathered.at[c], halo_s.at[5], halo_r.at[5], (s, face_of(y, x, 1 - c), r))
    d.start()
    copy_to(
        gathered.at[1 - c], gathered.at[1 - c], halo_s.at[5], halo_r.at[5], (s, f, r)
    ).wait_recv()

    def request(tile, m):
        k = 0 if m == 0 else 1
        j = r if m == 0 else m - 1
        u = links[tile, k]
        turn = turns[tile, k]
        odd = turn % 2
        half = j + odd - 2 * j * odd
        return u // 8, (u // 2) % 4, u % 2, 2 * (turn // 2) + half, odd

    for xd in range(4):
        tile = face_of(y, xd, c)
        for m in range(3):
            uy, ux, uc, q, odd = request(tile, m)
            chosen[xd, m] = gathered[uc, uy, q]

    arrived[x] = chosen[x]
    xsends = []
    for step in range(1, 4):
        xd = (x + step) % 4
        e = copy_to(
            chosen.at[xd], arrived.at[x], halo_s.at[5 + step], halo_r.at[5 + step], (s, face_of(y, xd, c), r)
        )
        e.start()
        xsends.append(e)
    for step in range(1, 4):
        xsrc = (x + 4 - step) % 4
        copy_to(
            chosen.at[x], arrived.at[xsrc], halo_s.at[5 + step], halo_r.at[5 + step], (s, f, r)
        ).wait_recv()
    for e in ysends + [d] + xsends:
        e.wait_send()

    turned = []
    ra = lax.broadcasted_iota(jnp.int32, (32, 32), 0)
    rb = lax.broadcasted_iota(jnp.int32, (32, 32), 1)
    for m in range(3):
        uy, ux, uc, q, odd = request(f, m)
        flip = jnp.where(rb == ra + odd * (23 - 2 * ra), 1.0, 0.0).astype(BF16)
        turned.append(jnp.dot(flip, arrived[ux, m], preferred_element_type=F32))
    east[...] = turned[0]
    at_top = jnp.full((24, BLK), r, jnp.int32) == 1
    north[0:24, :] = jnp.where(at_top, turned[1][0:24], inner[0].astype(F32)[0:24])
    north[24:48, :] = jnp.where(at_top, turned[2][0:24], inner[1].astype(F32)[0:24])

    eye = lax.broadcasted_iota(jnp.int32, (SIDE, SIDE), 0) == lax.broadcasted_iota(jnp.int32, (SIDE, SIDE), 1)
    last = lax.broadcasted_iota(jnp.int32, (SIDE, BLK), 0) == SIDE - 1
    lane = lax.broadcasted_iota(jnp.int32, (SIDE, LANE), 1)

    def column(row):
        return jnp.sum(jnp.where(eye, row, 0.0), axis=1, keepdims=True)

    def slope_row(i, acc):
        here = field[0, i].astype(F32)
        above = field[0, jnp.minimum(i + 1, ROWS - 1)].astype(F32)
        above = jnp.where(jnp.full((SIDE, BLK), i, jnp.int32) == ROWS - 1, north[...], above)
        right = jnp.where(last, east[pl.ds(i, 1), :], pltpu.roll(here, SIDE - 1, 0))
        gc = right - here
        gr = above - here
        inv = column(1.0 / area[0, pl.ds(i, 1), :])
        value = jnp.sqrt(1.0 + (gc * gc + gr * gr) * inv)
        slope[i] = value
        return jnp.where(lane == i, jnp.sum(value, axis=1, keepdims=True), acc)

    sums[s] = lax.fori_loop(0, ROWS, slope_row, jnp.zeros((SIDE, LANE), F32))
    psends = []
    for step in range(1, 4):
        e = copy_to(sums.at[s], sums.at[s], sum_s.at[step], sum_r.at[step], ((s + step) % 4, f, r))
        e.start()
        psends.append(e)
    for step in range(1, 4):
        src = (s + 4 - step) % 4
        copy_to(sums.at[src], sums.at[src], sum_s.at[step], sum_r.at[step], (s, f, r)).wait_recv()
    mean = (sums[0] + sums[1] + sums[2] + sums[3]) * (1.0 / SNAPS)
    for e in psends:
        e.wait_send()

    def anomaly_row(i, carry):
        m = jnp.sum(jnp.where(lane == i, mean, 0.0), axis=1, keepdims=True)
        w = column(jnp.sqrt(area[0, pl.ds(i, 1), :]) * mask[0, pl.ds(i, 1), :].astype(F32))
        value = (w * (slope[i] - m)).astype(BF16)
        anom[0, i] = value
        half = i // 12
        for k in range(4):
            own[k, half, i - 12 * half] = value[:, LANE * k : LANE * k + LANE]
        return carry

    lax.fori_loop(0, ROWS, anomaly_row, 0)

    def plane(mid):
        nb = 4 if mid else 3
        nt = nb - 1
        fmid = (other_mid, f, r)
        tend = (my_end, f, r)
        tmid = (my_mid, f, r)

        def chunk_of(k):
            return (k + y) % 4

        def send_own(k):
            kk = chunk_of(k)
            if mid:
                copy_to(own.at[kk, hfar], mid_in.at[kk], str_s.at[0, kk], mid_r.at[kk], fmid).start()
            else:
                copy_to(own.at[kk, hfar], end_in.at[kk, hfar], str_s.at[0, kk], end_r.at[kk, hfar], tmid).start()
                copy_to(own.at[kk, hnear], end_in.at[kk, hnear], str_s.at[1, kk], end_r.at[kk, hnear], tmid).start()

        def product(chunk, rows, acc):
            v = lax.dot_general(
                chunk.reshape(576, LANE),
                rows.reshape(576, BLK),
                (((0,), (0,)), ((), ())),
                preferred_element_type=F32,
            )
            return v if acc is None else acc + v

        def spread(k):
            kk = chunk_of(k)
            wait_bytes(take.at[k, 0 : 16 * (nb + nt)], pair_r.at[k])
            for b in range(nb):
                v = keep[k, 16 * b : 16 * b + 16] + take[k, 16 * b : 16 * b + 16].astype(F32)
                mixed_d[k, :, b] = v.astype(BF16)
            for b in range(nt):
                o = 16 * (nb + b)
                v = keep[k, o : o + 16] + take[k, o : o + 16].astype(F32)
                mixed_t[k, :, 4 * b : 4 * b + 4] = v.astype(BF16).reshape(4, 4, 16, LANE)
            red_d[kk, chip, 0:nb] = mixed_d[k, chip, 0:nb]

            def send_direct(step, carry):
                to = (chip + step) % 16
                copy_to(
                    mixed_d.at[k, to, 0:nb],
                    red_d.at[kk, chip, 0:nb],
                    dir_s.at[k],
                    dir_r.at[k],
                    (s, 2 * to + c, r),
                ).start()
                return carry

            lax.fori_loop(1, 16, send_direct, 0)

            def send_turned(step, carry):
                xd = (x + step) % 4
                copy_to(
                    mixed_t.at[k, xd, 0 : 4 * nt],
                    red_t.at[chip, 0 : 4 * nt],
                    tra_s.at[k],
                    tra_r.at[k],
                    (s, face_of(kk, xd, c), r),
                ).start()
                return carry

            lax.fori_loop(1, 4, send_turned, 0)

            @pl.when(k == 0)
            def _():
                red_t[chip, 0 : 4 * nt] = mixed_t[k, x, 0 : 4 * nt]

            @pl.when(k != 0)
            def _():
                send_turned(0, 0)

        send_own(0)
        send_own(1)

        def step(k, carry):
            kk = chunk_of(k)

            @pl.when(k < 2)
            def _():
                send_own(k + 2)

            if mid:
                ef = copy_to(end_in.at[kk, hfar], far_in.at[kk], str_s.at[1, kk], end_r.at[kk, hfar], fmid)
                ef.wait_recv()
                copy_to(end_in.at[kk, hfar], far_in.at[kk], str_s.at[1, kk], far_r.at[kk], fmid).start()
            wait_bytes(mid_in.at[kk], mid_r.at[kk])
            if mid:
                copy_to(mid_in.at[kk], mid_in.at[kk], str_s.at[2, kk], mid_r.at[kk], tend).start()
            wait_bytes(far_in.at[kk], far_r.at[kk])
            if mid:
                copy_to(far_in.at[kk], far_in.at[kk], str_s.at[3, kk], far_r.at[kk], tend).start()
                wait_bytes(end_in.at[kk, hnear], end_r.at[kk, hnear])
            near_rows = anom[0, pl.ds(12 * hnear, 12)]
            far_rows = anom[0, pl.ds(12 * hfar, 12)]
            results = [
                product(own[kk, hfar], far_rows, product(own[kk, hnear], near_rows, None)),
                product(mid_in[kk], near_rows, None),
                product(far_in[kk], near_rows, None),
            ]
            if mid:
                results.append(
                    product(end_in[kk, hfar], far_rows, product(end_in[kk, hnear], near_rows, None))
                )
            for b in range(nb):
                pt = results[b]
                p = jnp.transpose(pt).reshape(16, 2, 16, LANE)
                for core in range(2):
                    @pl.when(c == core)
                    def _():
                        keep[k, 16 * b : 16 * b + 16] = p[:, core]
                        give[k, 16 * b : 16 * b + 16] = p[:, 1 - core].astype(BF16)
                if b > 0:
                    o = 16 * (nb + b - 1)
                    pq = pt.reshape(4, 2, 16, BLK)
                    for core in range(2):
                        @pl.when(c == core)
                        def _():
                            for xd in range(4):
                                for l in range(4):
                                    ls = slice(LANE * l, LANE * l + LANE)
                                    keep[k, o + 4 * xd + l] = pq[xd, core, :, ls]
                                    give[k, o + 4 * xd + l] = pq[xd, 1 - core, :, ls].astype(BF16)
            copy_to(
                give.at[k, 0 : 16 * (nb + nt)],
                take.at[k, 0 : 16 * (nb + nt)],
                pair_s.at[k],
                pair_r.at[k],
                (s, face_of(y, x, 1 - c), r),
            ).start()

            @pl.when(k > 0)
            def _():
                spread(k - 1)

            return carry

        lax.fori_loop(0, 4, step, 0)
        spread(3)

        for k in range(4):
            wait_bytes(red_d.at[0, 0:15, 0:nb], dir_r.at[k])
            wait_bytes(red_t.at[0 : (3 if k == 0 else 4), 0 : 4 * nt], tra_r.at[k])

        for k in range(4):
            ls = slice(LANE * k, LANE * k + LANE)

            def add_direct(i, acc):
                return acc + red_d[k, i, 0:nb].astype(F32)

            total = lax.fori_loop(1, 16, add_direct, red_d[k, 0, 0:nb].astype(F32))
            for b in range(nb):
                piece_d[0, b, :, ls] = total[b, 0:8]
                piece_d[1, b, :, ls] = total[b, 8:16]
        def add_turned(i, acc):
            return acc + red_t[i, 0 : 4 * nt].astype(F32)

        total = lax.fori_loop(1, 16, add_turned, red_t[0, 0 : 4 * nt].astype(F32))
        for b in range(nt):
            for l in range(4):
                ls = slice(LANE * l, LANE * l + LANE)
                piece_t[0, b, :, ls] = total[4 * b + l, 0:8]
                piece_t[1, b, :, ls] = total[4 * b + l, 8:16]

        ends = []
        e = copy_to(piece_d.at[1 - r, 0:nb], fin_d.at[0:nb], fin_s.at[0], fin_r.at[0], (s, f, 1 - r))
        e.start()
        ends.append(e)
        others = [other_mid, other_end] + ([my_end] if mid else [])
        for b in range(nt):
            for q in range(2):
                e = copy_to(
                    piece_t.at[q, b],
                    fin_t.at[s, r],
                    fin_s.at[1 + 2 * b + q],
                    fin_r.at[1 + 2 * s + r],
                    (others[b], f, q),
                )
                e.start()
                ends.append(e)
        wait_bytes(fin_d.at[0:nb], fin_r.at[0])
        sources = [other_mid, other_end] + ([] if mid else [my_mid])
        for p in sources:
            for q in range(2):
                wait_bytes(fin_t.at[p, q], fin_r.at[1 + 2 * p + q])

        def put(block, value):
            gram[:, pl.ds(pl.multiple_of(block * BLK, BLK), BLK)] = value * GRAM_SCALE

        put(s, piece_d[r, 0] + fin_d[0])
        put(other_mid, piece_d[r, 1] + fin_d[1] + (fin_t[other_mid, 0] + fin_t[other_mid, 1]))
        put(other_end, piece_d[r, 2] + fin_d[2] + (fin_t[other_end, 0] + fin_t[other_end, 1]))
        if mid:
            put(my_end, piece_d[r, 3] + fin_d[3])
        else:
            put(my_mid, fin_t[my_mid, 0] + fin_t[my_mid, 1])

        for e in ends:
            e.wait_send()
        for k in range(4):
            wait_bytes(own.at[0, 0], str_s.at[0, k])
            wait_bytes(own.at[0, 0], str_s.at[1, k])
            if mid:
                wait_bytes(own.at[0, 0], str_s.at[2, k])
                wait_bytes(own.at[0, 0], str_s.at[3, k])
            wait_bytes(give.at[k, 0 : 16 * (nb + nt)], pair_s.at[k])
            wait_bytes(mixed_d.at[0, 0:15, 0:nb], dir_s.at[k])
            wait_bytes(red_t.at[0 : (3 if k == 0 else 4), 0 : 4 * nt], tra_s.at[k])

    @pl.when(is_mid)
    def _():
        plane(True)

    @pl.when(jnp.logical_not(is_mid))
    def _():
        plane(False)


def per_device(surface_field, ocean_mask, cell_area, tile_links, edge_turns):
    vmem = pl.BlockSpec(memory_space=pltpu.VMEM)
    smem = pl.BlockSpec(memory_space=pltpu.SMEM)
    dma = pltpu.SemaphoreType.DMA
    return pl.pallas_call(
        kernel,
        out_shape=(
            jax.ShapeDtypeStruct((1, ROWS, SIDE, BLK), BF16),
            jax.ShapeDtypeStruct((8, SNAPS), F32),
        ),
        in_specs=[smem, smem, vmem, vmem, vmem],
        out_specs=(vmem, vmem),
        scratch_shapes=[
            pltpu.VMEM((32, BLK), F32),
            pltpu.VMEM((4, 32, BLK), BF16),
            pltpu.VMEM((2, 32, BLK), BF16),
            pltpu.VMEM((2, 32, BLK), BF16),
            pltpu.VMEM((2, 4, 4, 32, BLK), BF16),
            pltpu.VMEM((4, 3, 32, BLK), BF16),
            pltpu.VMEM((4, 3, 32, BLK), BF16),
            pltpu.VMEM((32, BLK), F32),
            pltpu.VMEM((SIDE, BLK), F32),
            pltpu.VMEM((ROWS, SIDE, BLK), F32),
            pltpu.VMEM((4, SIDE, LANE), F32),
            pltpu.VMEM((4, 2, 12, SIDE, LANE), BF16),
            pltpu.VMEM((4, 2, 12, SIDE, LANE), BF16),
            pltpu.VMEM((4, 12, SIDE, LANE), BF16),
            pltpu.VMEM((4, 12, SIDE, LANE), BF16),
            pltpu.VMEM((4, 112, 16, LANE), F32),
            pltpu.VMEM((4, 112, 16, LANE), BF16),
            pltpu.VMEM((4, 112, 16, LANE), BF16),
            pltpu.VMEM((4, 16, 4, 16, LANE), BF16),
            pltpu.VMEM((4, 4, 12, 16, LANE), BF16),
            pltpu.VMEM((4, 16, 4, 16, LANE), BF16),
            pltpu.VMEM((16, 12, 16, LANE), BF16),
            pltpu.VMEM((2, 4, 8, BLK), F32),
            pltpu.VMEM((2, 3, 8, BLK), F32),
            pltpu.VMEM((4, 8, BLK), F32),
            pltpu.VMEM((4, 2, 8, BLK), F32),
            dma((9,)),
            dma((9,)),
            dma((4,)),
            dma((4,)),
            dma((4, 4)),
            dma((4, 2)),
            dma((4,)),
            dma((4,)),
            dma((4,)),
            dma((4,)),
            dma((4,)),
            dma((4,)),
            dma((4,)),
            dma((4,)),
            dma((7,)),
            dma((9,)),
        ],
        compiler_params=pltpu.CompilerParams(
            collective_id=0, has_side_effects=True, vmem_limit_bytes=56 * 1024 * 1024
        ),
        name="slope_gram",
    )(tile_links, edge_turns, surface_field, ocean_mask, cell_area)


def solution(mesh):
    placed = (
        P("face", "row", None, "snapshot"),
        P("face", "row", None),
        P("face", "row", None),
        P(),
        P(),
    )
    return jax.shard_map(
        per_device,
        mesh=mesh,
        in_specs=placed,
        out_specs=(P("face", "row", None, "snapshot"), P(("snapshot", "face", "row"), None)),
        check_vma=False,
    )
```

```python
import functools

import jax
import jax.numpy as jnp
from jax import lax
from jax.experimental import pallas as pl
from jax.experimental.pallas import tpu as pltpu
from jax.sharding import PartitionSpec as P

MESH = pl.DeviceIdType.MESH
BF16 = jnp.bfloat16
F32 = jnp.float32
SNAPS = 2048
ROWS = 24
SIDE = 48
BLK = 512
LANE = 128
GRAM_SCALE = 1.0 / (32 * 48 * 48)


def face_of(y, x, c):
    return (y * 4 + x) * 2 + c


def copy_to(src, dst, send_sem, recv_sem, device):
    return pltpu.make_async_remote_copy(
        src_ref=src,
        dst_ref=dst,
        send_sem=send_sem,
        recv_sem=recv_sem,
        device_id=device,
        device_id_type=MESH,
    )


def wait_bytes(ref, sem):
    pltpu.make_async_copy(ref, ref, sem).wait()


def kernel(
    links,
    field,
    mask,
    area,
    anom,
    gram,
    line_f,
    edge_f,
    halfw,
    otherw,
    others,
    lines,
    gathered,
    chosen,
    arrived,
    east,
    north,
    slope,
    slope_e,
    cells,
    sums,
    sums_e,
    shift,
    level,
    own,
    end_in,
    mid_in,
    far_in,
    edge_rows,
    edge_own,
    edge_end,
    edge_mid,
    edge_far,
    acc,
    keep,
    give,
    take,
    mixed_d,
    mixed_t,
    red_d,
    red_t,
    piece_d,
    piece_n,
    piece_t,
    mixed_n,
    fin_d,
    fin_n,
    fin_t,
    halo_s,
    halo_r,
    sum_s,
    sum_r,
    str_s,
    end_r,
    mid_r,
    far_r,
    edg_s,
    edg_r,
    pair_s,
    pair_r,
    dir_s,
    dir_r,
    tra_s,
    tra_r,
    fin_s,
    fin_r,
):
    s = lax.axis_index("snapshot")
    f = lax.axis_index("face")
    r = lax.axis_index("row")
    chip = f // 2
    c = f % 2
    y = chip // 4
    x = chip % 4
    side = s // 2
    is_mid = (s == 1) | (s == 2)
    my_mid = 1 + side
    my_end = 3 * side
    other_mid = 2 - side
    other_end = 3 - 3 * side
    hfar = side
    hnear = 1 - side
    at_mid = (other_mid, f, r)
    at_end = (my_end, f, r)
    at_my_mid = (my_mid, f, r)
    at_core = (s, face_of(y, x, 1 - c), r)

    def on_mid(do):
        pl.when(is_mid)(do)

    def on_end(do):
        pl.when(jnp.logical_not(is_mid))(do)

    def chunk_of(k):
        return (k + y) % 4

    barrier = pltpu.get_barrier_semaphore()

    def greet(device):
        pl.semaphore_signal(barrier, inc=1, device_id=device, device_id_type=MESH)

    greet((s, f, 1 - r))
    greet(at_core)

    def greet_chip(step, carry):
        greet((s, 2 * ((chip + step) % 16) + c, r))
        return carry

    lax.fori_loop(1, 16, greet_chip, 0)

    def greet_plane(step, carry):
        greet(((s + step) % 4, f, r))
        greet(((s + step) % 4, f, 1 - r))
        return carry

    lax.fori_loop(1, 4, greet_plane, 0)

    eye = lax.broadcasted_iota(jnp.int32, (SIDE, SIDE), 0) == lax.broadcasted_iota(jnp.int32, (SIDE, SIDE), 1)
    last = lax.broadcasted_iota(jnp.int32, (SIDE, BLK), 0) == SIDE - 1
    inside = lax.broadcasted_iota(jnp.int32, (SIDE, 1), 0) < SIDE - 1
    lane = lax.broadcasted_iota(jnp.int32, (SIDE, LANE), 1)

    def column(row):
        return jnp.sum(jnp.where(eye, row, 0.0), axis=1, keepdims=True)

    def weight_row(i):
        return jnp.sqrt(area[0, pl.ds(i, 1), :]) * mask[0, pl.ds(i, 1), :].astype(F32)

    def steepness(gc, gr, inv):
        return jnp.sqrt(1.0 + (gc * gc + gr * gr) * inv)

    def inner_row(i, carry):
        total, weights = carry
        here = field[0, i].astype(F32)
        above = field[0, i + 1].astype(F32)
        value = steepness(pltpu.roll(here, SIDE - 1, 0) - here, above - here, column(1.0 / area[0, pl.ds(i, 1), :]))
        slope[i] = value
        sv = jnp.sum(value, axis=1, keepdims=True)
        w = jnp.where(inside, column(weight_row(i)), 0.0)
        out = (w * (value - sv * (1.0 / BLK))).astype(BF16)
        half = i // 11
        for k in range(4):
            own[k, half, i - 11 * half] = out[:, LANE * k : LANE * k + LANE]
        return jnp.where(lane == i, sv, total), jnp.where(lane == i, w, weights)

    zero = jnp.zeros((SIDE, LANE), F32)
    total, weights = lax.fori_loop(0, 22, inner_row, (zero, zero))
    sums[s] = total

    line_f[...] = jnp.zeros_like(line_f)
    for i in range(ROWS):
        line_f[i : i + 1, :] = field[0, i, 0:16, :].astype(F32)[0:1]
        edge_f[i : i + 1, :] = field[0, i, 32:48, :].astype(F32)[15:16]
    halfw[...] = line_f[...].astype(BF16)

    pl.semaphore_wait(barrier, 23)

    other_row = (s, f, 1 - r)
    za = copy_to(halfw, otherw, halo_s.at[0], halo_r.at[0], other_row)
    zb = copy_to(field.at[0, 0], others, halo_s.at[1], halo_r.at[1], other_row)
    za.start()
    zb.start()

    def send_sums(ref, n):
        for step in range(1, 4):
            copy_to(ref.at[s], ref.at[s], sum_s.at[n, step], sum_r.at[n, step], ((s + step) % 4, f, r)).start()

    def wait_sums(ref, n):
        for step in range(1, 4):
            wait_bytes(ref.at[0], sum_r.at[n, step])
        for step in range(1, 4):
            wait_bytes(ref.at[0], sum_s.at[n, step])

    def send_own(k):
        kk = chunk_of(k)

        @on_mid
        def _():
            copy_to(own.at[kk, hfar], mid_in.at[kk], str_s.at[0, kk], mid_r.at[kk], at_mid).start()

        @on_end
        def _():
            copy_to(own.at[kk, hfar], end_in.at[kk, hfar], str_s.at[0, kk], end_r.at[kk, hfar], at_my_mid).start()
            copy_to(own.at[kk, hnear], end_in.at[kk, hnear], str_s.at[1, kk], end_r.at[kk, hnear], at_my_mid).start()

    def pass_end(k):
        @on_mid
        def _():
            kk = chunk_of(k)
            wait_bytes(end_in.at[kk, hfar], end_r.at[kk, hfar])
            copy_to(end_in.at[kk, hfar], far_in.at[kk], str_s.at[1, kk], far_r.at[kk], at_mid).start()

    def pass_mid(k):
        @on_mid
        def _():
            kk = chunk_of(k)
            wait_bytes(mid_in.at[kk], mid_r.at[kk])
            copy_to(mid_in.at[kk], mid_in.at[kk], str_s.at[2, kk], mid_r.at[kk], at_end).start()

    def pass_far(k):
        @on_mid
        def _():
            kk = chunk_of(k)
            wait_bytes(far_in.at[kk], far_r.at[kk])
            copy_to(far_in.at[kk], far_in.at[kk], str_s.at[3, kk], far_r.at[kk], at_end).start()

    send_sums(sums, 0)
    send_own(0)
    send_own(1)

    za.wait_recv()
    zb.wait_recv()
    low = jnp.full((ROWS, BLK), r, jnp.int32) == 0
    wa = line_f[0:ROWS]
    wb = otherw[...].astype(F32)[0:ROWS]
    west = jnp.concatenate([jnp.where(low, wa, wb), jnp.where(low, wb, wa)], axis=0).astype(BF16)
    south = jnp.where(
        jnp.full((SIDE, BLK), r, jnp.int32) == 0, field[0, 0].astype(F32), others[...].astype(F32)
    ).astype(BF16)

    def place(p, a, b):
        return face_of(a, b, c) if p == 0 else face_of(b, a, c)

    here_on = [(y, x), (x, y)]
    for p in range(2):
        a, b = here_on[p]
        ls = slice(256 * p, 256 * p + 256)
        lines[p, 0] = west[:, ls]
        lines[p, 1] = south[:, ls]
        gathered[p, c, a, 0] = west[:, ls]
        gathered[p, c, a, 1] = south[:, ls]
        for step in range(1, 4):
            n = 1 + 3 * p + step
            copy_to(
                lines.at[p], gathered.at[p, c, a], halo_s.at[n], halo_r.at[n], (s, place(p, (a + step) % 4, b), r)
            ).start()

    wait_sums(sums, 0)
    mean = (sums[0] + sums[1] + sums[2] + sums[3]) * (1.0 / SNAPS)
    sources = [other_mid, other_end, my_end]
    deltas = [weights * (sums[p] * (1.0 / BLK) - mean) for p in sources]

    def pick(matrix, i):
        return jnp.sum(jnp.where(lane == i, matrix, 0.0), axis=1, keepdims=True)

    def inner_anomaly(i, carry):
        w = column(weight_row(i))
        anom[0, i] = (w * (slope[i] - pick(mean, i))).astype(BF16)
        for b in range(3):
            shift[b, i] = jnp.broadcast_to(pick(deltas[b], i), (SIDE, LANE)).astype(BF16)
        return carry

    lax.fori_loop(0, 22, inner_anomaly, 0)
    pass_end(0)
    pass_mid(0)

    for p in range(2):
        a, b = here_on[p]
        for step in range(1, 4):
            wait_bytes(lines.at[p], halo_r.at[1 + 3 * p + step])
        copy_to(gathered.at[p, c], gathered.at[p, c], halo_s.at[8 + p], halo_r.at[8 + p], at_core).start()
    pass_far(0)

    def request(tile, side_index):
        u = links[2 * tile + side_index]
        turn = links[64 + 2 * tile + side_index]
        return u // 8, (u // 2) % 4, u % 2, turn // 2, turn % 2

    for p in range(2):
        wait_bytes(gathered.at[p, 0], halo_r.at[8 + p])
    for p in range(2):
        a, b = here_on[p]
        for bd in range(4):
            for m in range(2):
                uy, ux, uc, q, odd = request(place(p, a, bd), m)
                chosen[p, bd, m] = gathered[p, uc, uy if p == 0 else ux, q]
        arrived[p, b] = chosen[p, b]
        for step in range(1, 4):
            bd = (b + step) % 4
            n = 9 + 3 * p + step
            to = (s, place(p, a, bd), r)
            copy_to(chosen.at[p, bd, 0], arrived.at[p, b, 0], halo_s.at[n], halo_r.at[n], to).start()

            @pl.when(r == 1)
            def _():
                copy_to(chosen.at[p, bd, 1], arrived.at[p, b, 1], halo_s.at[n + 6], halo_r.at[n + 6], to).start()

    send_own(2)
    pass_end(1)
    pass_mid(1)

    def product(chunk, rows):
        k_size = chunk.shape[0] * chunk.shape[1]
        return lax.dot_general(
            chunk.reshape(k_size, LANE),
            rows.reshape(k_size, BLK),
            (((0,), (0,)), ((), ())),
            preferred_element_type=F32,
        )

    def inner_product(chunk, h):
        return product(chunk[...], anom[0, pl.ds(11 * h, 11)])

    def own_product(kk):
        cols = anom[0, 0:22, :, pl.ds(pl.multiple_of(kk * LANE, LANE), LANE)]
        live = lax.broadcasted_iota(jnp.int32, (22, SIDE, LANE), 1) < SIDE - 1
        cols = jnp.where(live, cols.astype(F32), 0.0).astype(BF16)
        return product(cols, anom[0, 0:22])

    near_inner = pl.ds(11 * hnear, 11)
    level[0] = product(shift[0, near_inner], anom[0, near_inner])
    level[1] = product(shift[1, near_inner], anom[0, near_inner])

    @on_mid
    def _():
        level[2] = product(shift[2], anom[0, 0:22])

    def products(k):
        kk = chunk_of(k)
        acc[0, k] = own_product(kk)

        @on_end
        def _():
            wait_bytes(mid_in.at[kk], mid_r.at[kk])
            wait_bytes(far_in.at[kk], far_r.at[kk])

        acc[1, k] = inner_product(mid_in.at[kk], hnear) + level[0]
        acc[2, k] = inner_product(far_in.at[kk], hnear) + level[1]

        @on_mid
        def _():
            wait_bytes(end_in.at[kk, hnear], end_r.at[kk, hnear])
            acc[3, k] = inner_product(end_in.at[kk, 0], 0) + inner_product(end_in.at[kk, 1], 1) + level[2]

    products(0)

    for p in range(2):
        for step in range(1, 4):
            n = 9 + 3 * p + step
            wait_bytes(arrived.at[0, 0, 0], halo_r.at[n])

            @pl.when(r == 1)
            def _():
                wait_bytes(arrived.at[0, 0, 0], halo_r.at[n + 6])

    row_id = lax.broadcasted_iota(jnp.int32, (SIDE, SIDE), 0)
    col_id = lax.broadcasted_iota(jnp.int32, (SIDE, SIDE), 1)
    for p in range(2):
        ls = slice(256 * p, 256 * p + 256)
        uy, ux, uc, q, odd = request(f, 0)
        cell = row_id[0:32] + 24 * r
        flip = jnp.where(col_id[0:32] == cell + odd * (47 - 2 * cell), 1.0, 0.0).astype(BF16)
        east[:, ls] = jnp.dot(flip, arrived[p, ux if p == 0 else uy, 0], preferred_element_type=F32)

        @pl.when(r == 1)
        def _():
            uy, ux, uc, q, odd = request(f, 1)
            flip = jnp.where(col_id == row_id + odd * (47 - 2 * row_id), 1.0, 0.0).astype(BF16)
            north[:, ls] = jnp.dot(flip, arrived[p, ux if p == 0 else uy, 1], preferred_element_type=F32)

    @pl.when(r == 0)
    def _():
        north[...] = others[...].astype(F32)

    esum = zero
    for h in range(2):
        i = 22 + h
        here = field[0, i].astype(F32)
        above = north[...] if h else field[0, i + 1].astype(F32)
        right = jnp.where(last, east[i : i + 1, :], pltpu.roll(here, SIDE - 1, 0))
        value = steepness(right - here, above - here, column(1.0 / area[0, i : i + 1, :]))
        slope[i] = value
        esum = jnp.where(lane == h, jnp.sum(value, axis=1, keepdims=True), esum)
    ecol = edge_f[...]
    esteep = steepness(
        east[0:ROWS] - ecol, pltpu.roll(ecol, ROWS - 1, 0) - ecol, 1.0 / area[0][:, SIDE - 1 : SIDE]
    )
    slope_e[...] = esteep
    colsum = jnp.concatenate(
        [jnp.sum(esteep, axis=1, keepdims=True), jnp.zeros((SIDE - ROWS, 1), F32)], axis=0
    )
    sums_e[s] = jnp.where(lane == 2, colsum, esum)
    send_sums(sums_e, 1)
    pass_far(1)
    products(1)

    wait_sums(sums_e, 1)
    emean = (sums_e[0] + sums_e[1] + sums_e[2] + sums_e[3]) * (1.0 / SNAPS)
    ew = jnp.sqrt(area[0][:, SIDE - 1 : SIDE]) * mask[0][:, SIDE - 1 : SIDE].astype(F32)
    evalue = ew * (slope_e[...] - pick(emean, 2)[0:ROWS])
    slope_e[...] = evalue
    cells[...] = jnp.zeros_like(cells)
    for h in range(2):
        i = 22 + h
        cells[h, 0:SIDE] = column(weight_row(i)) * (slope[i] - pick(emean, h))
        cells[h, SIDE : SIDE + 11] = evalue[11 * h : 11 * h + 11]
        both = cells[h].astype(BF16)
        anom[0, i] = both[0:SIDE]
        edge_rows[h] = both
        for k in range(4):
            edge_own[h, k] = both[:, LANE * k : LANE * k + LANE]

    @on_mid
    def _():
        copy_to(edge_own.at[hfar], edge_mid, edg_s.at[0], edg_r.at[2], at_mid).start()

    @on_end
    def _():
        copy_to(edge_own.at[hfar], edge_end.at[hfar], edg_s.at[0], edg_r.at[hfar], at_my_mid).start()
        copy_to(edge_own.at[hnear], edge_end.at[hnear], edg_s.at[1], edg_r.at[hnear], at_my_mid).start()

    send_own(3)

    def put_column(i, carry):
        tile = anom[0, i, 32:48].astype(F32)
        at = lax.broadcasted_iota(jnp.int32, (16, BLK), 0) == 15
        anom[0, i, 32:48] = jnp.where(at, slope_e[pl.ds(i, 1), :], tile).astype(BF16)
        return carry

    pass_end(2)
    pass_mid(2)
    pass_far(2)

    @on_mid
    def _():
        wait_bytes(edge_end.at[0], edg_r.at[hfar])
        copy_to(edge_end.at[hfar], edge_far, edg_s.at[1], edg_r.at[3], at_mid).start()
        wait_bytes(edge_mid, edg_r.at[2])
        copy_to(edge_mid, edge_mid, edg_s.at[2], edg_r.at[2], at_end).start()

    products(2)
    pass_end(3)

    @on_mid
    def _():
        wait_bytes(edge_far, edg_r.at[3])
        copy_to(edge_far, edge_far, edg_s.at[3], edg_r.at[3], at_end).start()
        wait_bytes(edge_end.at[0], edg_r.at[hnear])

    @on_end
    def _():
        wait_bytes(edge_mid, edg_r.at[2])
        wait_bytes(edge_far, edg_r.at[3])

    def plane(mid):
        nb = 4 if mid else 3
        nt = nb - 1

        def emit(k):
            kk = chunk_of(k)
            near_edge = edge_rows[hnear]
            extra = [
                product(edge_own[:, kk], edge_rows[...]),
                product(edge_mid[kk][None], near_edge[None]),
                product(edge_far[kk][None], near_edge[None]),
            ]
            if mid:
                extra.append(product(edge_end[:, kk], edge_rows[...]))
            for b in range(nb):
                pt = acc[b, k] + extra[b]
                p = jnp.transpose(pt).reshape(16, 2, 16, LANE)
                for core in range(2):
                    @pl.when(c == core)
                    def _():
                        keep[k, 16 * b : 16 * b + 16] = p[:, core]
                        give[k, 16 * b : 16 * b + 16] = p[:, 1 - core].astype(BF16)
                if b > 0:
                    o = 16 * (nb + b - 1)
                    pq = pt.reshape(4, 2, 16, BLK)
                    for core in range(2):
                        @pl.when(c == core)
                        def _():
                            for xd in range(4):
                                for l in range(4):
                                    ls = slice(LANE * l, LANE * l + LANE)
                                    keep[k, o + 4 * xd + l] = pq[xd, core, :, ls]
                                    give[k, o + 4 * xd + l] = pq[xd, 1 - core, :, ls].astype(BF16)
            copy_to(
                give.at[k, 0 : 16 * (nb + nt)],
                take.at[k, 0 : 16 * (nb + nt)],
                pair_s.at[k],
                pair_r.at[k],
                at_core,
            ).start()

        def spread(k):
            kk = chunk_of(k)
            wait_bytes(take.at[k, 0 : 16 * (nb + nt)], pair_r.at[k])
            for b in range(nb):
                v = keep[k, 16 * b : 16 * b + 16] + take[k, 16 * b : 16 * b + 16].astype(F32)
                mixed_d[k, :, b] = v.astype(BF16)
            for b in range(nt):
                o = 16 * (nb + b)
                v = keep[k, o : o + 16] + take[k, o : o + 16].astype(F32)
                mixed_t[k, :, 4 * b : 4 * b + 4] = v.astype(BF16).reshape(4, 4, 16, LANE)
            red_d[kk, chip, 0:nb] = mixed_d[k, chip, 0:nb]

            def send_direct(step, carry):
                to = (chip + step) % 16
                copy_to(
                    mixed_d.at[k, to, 0:nb],
                    red_d.at[kk, chip, 0:nb],
                    dir_s.at[k],
                    dir_r.at[k],
                    (s, 2 * to + c, r),
                ).start()
                return carry

            lax.fori_loop(1, 16, send_direct, 0)

            def send_turned(step, carry):
                xd = (x + step) % 4
                copy_to(
                    mixed_t.at[k, xd, 0 : 4 * nt],
                    red_t.at[chip, 0 : 4 * nt],
                    tra_s.at[k],
                    tra_r.at[k],
                    (s, face_of(kk, xd, c), r),
                ).start()
                return carry

            lax.fori_loop(1, 4, send_turned, 0)

            @pl.when(k == 0)
            def _():
                red_t[chip, 0 : 4 * nt] = mixed_t[k, x, 0 : 4 * nt]

            @pl.when(k != 0)
            def _():
                send_turned(0, 0)

        def turn(k, carry):
            emit(k)

            @pl.when(k > 0)
            def _():
                spread(k - 1)

            @pl.when(k == 1)
            def _():
                pass_mid(3)
                pass_far(3)

            @pl.when(k == 2)
            def _():
                products(3)

            return carry

        lax.fori_loop(0, 4, turn, 0)
        lax.fori_loop(0, 22, put_column, 0)
        spread(3)

        for k in range(4):
            wait_bytes(red_d.at[0, 0:15, 0:nb], dir_r.at[k])
            wait_bytes(red_t.at[0 : (3 if k == 0 else 4), 0 : 4 * nt], tra_r.at[k])

        for k in range(4):
            ls = slice(LANE * k, LANE * k + LANE)
            ln = slice(LANE * (k % 2), LANE * (k % 2) + LANE)
            rn = slice(8 * (k // 2), 8 * (k // 2) + 8)

            def add_direct(i, acc):
                return acc + red_d[k, i, 0:nb].astype(F32)

            total = lax.fori_loop(1, 16, add_direct, red_d[k, 0, 0:nb].astype(F32))
            for q in range(2):
                piece_d[q, :, ls] = total[0, 8 * q : 8 * q + 8]
                for b in range(nt):
                    piece_n[q, b, rn, ln] = total[1 + b, 8 * q : 8 * q + 8]

        def add_turned(i, acc):
            return acc + red_t[i, 0 : 4 * nt].astype(F32)

        total = lax.fori_loop(1, 16, add_turned, red_t[0, 0 : 4 * nt].astype(F32))
        for b in range(nt):
            for q in range(2):
                rows = slice(8 * q, 8 * q + 8)
                parts = [total[4 * b + l, rows] for l in range(4)]
                top = jnp.concatenate(parts[0:2], axis=1)
                bottom = jnp.concatenate(parts[2:4], axis=1)
                piece_t[q, b] = jnp.concatenate([top, bottom], axis=0).astype(BF16)
        for b in range(nt):
            mixed_n[b] = piece_n[1 - r, b].astype(BF16)

        ends = []
        e = copy_to(piece_d.at[1 - r], fin_d, fin_s.at[0], fin_r.at[0], other_row)
        e.start()
        ends.append(e)
        e = copy_to(mixed_n.at[0:nt], fin_n.at[0:nt], fin_s.at[7], fin_r.at[9], other_row)
        e.start()
        ends.append(e)
        others_of = [other_mid, other_end] + ([my_end] if mid else [])
        for b in range(nt):
            for q in range(2):
                e = copy_to(
                    piece_t.at[q, b],
                    fin_t.at[s, r],
                    fin_s.at[1 + 2 * b + q],
                    fin_r.at[1 + 2 * s + r],
                    (others_of[b], f, q),
                )
                e.start()
                ends.append(e)
        wait_bytes(fin_d, fin_r.at[0])
        wait_bytes(fin_n.at[0:nt], fin_r.at[9])
        sources = [other_mid, other_end] + ([] if mid else [my_mid])
        for p in sources:
            for q in range(2):
                wait_bytes(fin_t.at[p, q], fin_r.at[1 + 2 * p + q])

        def put(block, value):
            gram[:, pl.ds(pl.multiple_of(block * BLK, BLK), BLK)] = value * GRAM_SCALE

        def put_folded(block, value):
            put(block, jnp.concatenate([value[0:8], value[8:16]], axis=1))

        def turned(p):
            return fin_t[p, 0].astype(F32) + fin_t[p, 1].astype(F32)

        def straight(b):
            return piece_n[r, b] + fin_n[b].astype(F32)

        put(s, piece_d[r] + fin_d[...])
        put_folded(other_mid, straight(0) + turned(other_mid))
        put_folded(other_end, straight(1) + turned(other_end))
        if mid:
            put_folded(my_end, straight(2))
        else:
            put_folded(my_mid, turned(my_mid))

        for e in ends:
            e.wait_send()
        for k in range(4):
            wait_bytes(own.at[0, 0], str_s.at[0, k])
            wait_bytes(own.at[0, 0], str_s.at[1, k])
            if mid:
                wait_bytes(own.at[0, 0], str_s.at[2, k])
                wait_bytes(own.at[0, 0], str_s.at[3, k])
            wait_bytes(edge_own.at[0], edg_s.at[k]) if mid or k < 2 else None
            wait_bytes(give.at[k, 0 : 16 * (nb + nt)], pair_s.at[k])
            wait_bytes(mixed_d.at[0, 0:15, 0:nb], dir_s.at[k])
            wait_bytes(red_t.at[0 : (3 if k == 0 else 4), 0 : 4 * nt], tra_s.at[k])

    @on_mid
    def _():
        plane(True)

    @on_end
    def _():
        plane(False)

    za.wait_send()
    zb.wait_send()
    for p in range(2):
        for step in range(1, 4):
            wait_bytes(lines.at[p], halo_s.at[1 + 3 * p + step])
            wait_bytes(arrived.at[0, 0, 0], halo_s.at[9 + 3 * p + step])

            @pl.when(r == 1)
            def _():
                wait_bytes(arrived.at[0, 0, 0], halo_s.at[15 + 3 * p + step])

        wait_bytes(gathered.at[p, 0], halo_s.at[8 + p])


def per_device(surface_field, ocean_mask, cell_area, tile_links, edge_turns):
    vmem = pl.BlockSpec(memory_space=pltpu.VMEM)
    smem = pl.BlockSpec(memory_space=pltpu.SMEM)
    dma = pltpu.SemaphoreType.DMA
    links = jnp.concatenate([tile_links.reshape(-1), edge_turns.reshape(-1)])
    return pl.pallas_call(
        kernel,
        out_shape=(
            jax.ShapeDtypeStruct((1, ROWS, SIDE, BLK), BF16),
            jax.ShapeDtypeStruct((8, SNAPS), F32),
        ),
        in_specs=[smem, vmem, vmem, vmem],
        out_specs=(vmem, vmem),
        scratch_shapes=[
            pltpu.VMEM((32, BLK), F32),
            pltpu.VMEM((ROWS, BLK), F32),
            pltpu.VMEM((32, BLK), BF16),
            pltpu.VMEM((32, BLK), BF16),
            pltpu.VMEM((SIDE, BLK), BF16),
            pltpu.VMEM((2, 2, SIDE, 256), BF16),
            pltpu.VMEM((2, 2, 4, 2, SIDE, 256), BF16),
            pltpu.VMEM((2, 4, 2, SIDE, 256), BF16),
            pltpu.VMEM((2, 4, 2, SIDE, 256), BF16),
            pltpu.VMEM((32, BLK), F32),
            pltpu.VMEM((SIDE, BLK), F32),
            pltpu.VMEM((ROWS, SIDE, BLK), F32),
            pltpu.VMEM((ROWS, BLK), F32),
            pltpu.VMEM((2, 64, BLK), F32),
            pltpu.VMEM((4, SIDE, LANE), F32),
            pltpu.VMEM((4, SIDE, LANE), F32),
            pltpu.VMEM((3, 22, SIDE, LANE), BF16),
            pltpu.VMEM((3, LANE, BLK), F32),
            pltpu.VMEM((4, 2, 11, SIDE, LANE), BF16),
            pltpu.VMEM((4, 2, 11, SIDE, LANE), BF16),
            pltpu.VMEM((4, 11, SIDE, LANE), BF16),
            pltpu.VMEM((4, 11, SIDE, LANE), BF16),
            pltpu.VMEM((2, 64, BLK), BF16),
            pltpu.VMEM((2, 4, 64, LANE), BF16),
            pltpu.VMEM((2, 4, 64, LANE), BF16),
            pltpu.VMEM((4, 64, LANE), BF16),
            pltpu.VMEM((4, 64, LANE), BF16),
            pltpu.VMEM((4, 4, LANE, BLK), F32),
            pltpu.VMEM((4, 112, 16, LANE), F32),
            pltpu.VMEM((4, 112, 16, LANE), BF16),
            pltpu.VMEM((4, 112, 16, LANE), BF16),
            pltpu.VMEM((4, 16, 4, 16, LANE), BF16),
            pltpu.VMEM((4, 4, 12, 16, LANE), BF16),
            pltpu.VMEM((4, 16, 4, 16, LANE), BF16),
            pltpu.VMEM((16, 12, 16, LANE), BF16),
            pltpu.VMEM((2, 8, BLK), F32),
            pltpu.VMEM((2, 3, 16, 256), F32),
            pltpu.VMEM((2, 3, 16, 256), BF16),
            pltpu.VMEM((3, 16, 256), BF16),
            pltpu.VMEM((8, BLK), F32),
            pltpu.VMEM((3, 16, 256), BF16),
            pltpu.VMEM((4, 2, 16, 256), BF16),
            dma((22,)),
            dma((22,)),
            dma((2, 4)),
            dma((2, 4)),
            dma((4, 4)),
            dma((4, 2)),
            dma((4,)),
            dma((4,)),
            dma((4,)),
            dma((4,)),
            dma((4,)),
            dma((4,)),
            dma((4,)),
            dma((4,)),
            dma((4,)),
            dma((4,)),
            dma((8,)),
            dma((10,)),
        ],
        compiler_params=pltpu.CompilerParams(
            collective_id=0, has_side_effects=True, vmem_limit_bytes=56 * 1024 * 1024
        ),
        name="slope_gram",
    )(links, surface_field, ocean_mask, cell_area)


def solution(mesh):
    placed = (
        P("face", "row", None, "snapshot"),
        P("face", "row", None),
        P("face", "row", None),
        P(),
        P(),
    )
    return jax.shard_map(
        per_device,
        mesh=mesh,
        in_specs=placed,
        out_specs=(P("face", "row", None, "snapshot"), P(("snapshot", "face", "row"), None)),
        check_vma=False,
    )
```

```python
import functools

import jax
import jax.numpy as jnp
from jax import lax
from jax.experimental import pallas as pl
from jax.experimental.pallas import tpu as pltpu
from jax.sharding import PartitionSpec as P

MESH = pl.DeviceIdType.MESH
BF16 = jnp.bfloat16
F32 = jnp.float32
SNAPS = 2048
ROWS = 24
SIDE = 48
BLK = 512
LANE = 128
GRAM_SCALE = 1.0 / (32 * 48 * 48)


def face_of(y, x, c):
    return (y * 4 + x) * 2 + c


def copy_to(src, dst, send_sem, recv_sem, device):
    return pltpu.make_async_remote_copy(
        src_ref=src,
        dst_ref=dst,
        send_sem=send_sem,
        recv_sem=recv_sem,
        device_id=device,
        device_id_type=MESH,
    )


def wait_bytes(ref, sem):
    pltpu.make_async_copy(ref, ref, sem).wait()


def kernel(
    links,
    field,
    mask,
    area,
    anom,
    gram,
    line_f,
    edge_f,
    halfw,
    otherw,
    others,
    lines,
    gathered,
    chosen,
    arrived,
    east,
    north,
    slope,
    slope_e,
    cells,
    sums,
    sums_e,
    shift,
    shift_e,
    level,
    own,
    end_in,
    mid_in,
    far_in,
    edge_rows,
    edge_own,
    edge_end,
    edge_mid,
    edge_far,
    acc,
    keep,
    give,
    take,
    mixed_d,
    mixed_t,
    red_d,
    red_t,
    tot,
    piece_d,
    piece_n,
    piece_t,
    mixed_n,
    fin_d,
    fin_n,
    fin_t,
    halo_s,
    halo_r,
    sum_s,
    sum_r,
    str_s,
    end_r,
    mid_r,
    far_r,
    edg_s,
    edg_r,
    pair_s,
    pair_r,
    dir_s,
    dir_r,
    tra_s,
    tra_r,
    fin_s,
    fin_r,
):
    s = lax.axis_index("snapshot")
    f = lax.axis_index("face")
    r = lax.axis_index("row")
    chip = f // 2
    c = f % 2
    y = chip // 4
    x = chip % 4
    side = s // 2
    is_mid = (s == 1) | (s == 2)
    my_mid = 1 + side
    my_end = 3 * side
    other_mid = 2 - side
    other_end = 3 - 3 * side
    hfar = side
    hnear = 1 - side
    at_mid = (other_mid, f, r)
    at_end = (my_end, f, r)
    at_my_mid = (my_mid, f, r)
    at_core = (s, face_of(y, x, 1 - c), r)

    def on_mid(do):
        pl.when(is_mid)(do)

    def on_end(do):
        pl.when(jnp.logical_not(is_mid))(do)

    def chunk_of(k):
        return (k + y) % 4

    barrier = pltpu.get_barrier_semaphore()

    def greet(device):
        pl.semaphore_signal(barrier, inc=1, device_id=device, device_id_type=MESH)

    greet((s, f, 1 - r))
    greet(at_core)

    def greet_chip(step, carry):
        greet((s, 2 * ((chip + step) % 16) + c, r))
        return carry

    lax.fori_loop(1, 16, greet_chip, 0)

    def greet_plane(step, carry):
        greet(((s + step) % 4, f, r))
        greet(((s + step) % 4, f, 1 - r))
        return carry

    lax.fori_loop(1, 4, greet_plane, 0)

    eye = lax.broadcasted_iota(jnp.int32, (SIDE, SIDE), 0) == lax.broadcasted_iota(jnp.int32, (SIDE, SIDE), 1)
    last = lax.broadcasted_iota(jnp.int32, (SIDE, BLK), 0) == SIDE - 1
    inside = lax.broadcasted_iota(jnp.int32, (SIDE, 1), 0) < SIDE - 1
    lane = lax.broadcasted_iota(jnp.int32, (SIDE, LANE), 1)

    def column(row):
        return jnp.sum(jnp.where(eye, row, 0.0), axis=1, keepdims=True)

    def weight_row(i):
        return jnp.sqrt(area[0, pl.ds(i, 1), :]) * mask[0, pl.ds(i, 1), :].astype(F32)

    def steepness(gc, gr, inv):
        return jnp.sqrt(1.0 + (gc * gc + gr * gr) * inv)

    def inner_row(i, carry):
        total, weights = carry
        here = field[0, i].astype(F32)
        above = field[0, i + 1].astype(F32)
        value = steepness(pltpu.roll(here, SIDE - 1, 0) - here, above - here, column(1.0 / area[0, pl.ds(i, 1), :]))
        slope[i] = value
        sv = jnp.sum(value, axis=1, keepdims=True)
        w = jnp.where(inside, column(weight_row(i)), 0.0)
        out = (w * (value - sv * (1.0 / BLK))).astype(BF16)
        half = i // 11
        for k in range(4):
            own[k, half, i - 11 * half] = out[:, LANE * k : LANE * k + LANE]
        return jnp.where(lane == i, sv, total), jnp.where(lane == i, w, weights)

    zero = jnp.zeros((SIDE, LANE), F32)
    total, weights = lax.fori_loop(0, 22, inner_row, (zero, zero))
    sums[s] = total

    line_f[...] = jnp.zeros_like(line_f)
    for i in range(ROWS):
        line_f[i : i + 1, :] = field[0, i, 0:16, :].astype(F32)[0:1]
        edge_f[i : i + 1, :] = field[0, i, 32:48, :].astype(F32)[15:16]
    halfw[...] = line_f[...].astype(BF16)

    pl.semaphore_wait(barrier, 23)

    other_row = (s, f, 1 - r)
    za = copy_to(halfw, otherw, halo_s.at[0], halo_r.at[0], other_row)
    zb = copy_to(field.at[0, 0], others, halo_s.at[1], halo_r.at[1], other_row)
    za.start()
    zb.start()

    def send_sums(ref, n):
        for step in range(1, 4):
            copy_to(ref.at[s], ref.at[s], sum_s.at[n, step], sum_r.at[n, step], ((s + step) % 4, f, r)).start()

    def wait_sums(ref, n):
        for step in range(1, 4):
            wait_bytes(ref.at[0], sum_r.at[n, step])
        for step in range(1, 4):
            wait_bytes(ref.at[0], sum_s.at[n, step])

    def send_mid(k):
        @on_mid
        def _():
            kk = chunk_of(k)
            copy_to(own.at[kk, hfar], mid_in.at[kk], str_s.at[0, kk], mid_r.at[kk], at_mid).start()

    def send_end(n):
        @on_end
        def _():
            if n >= 2:
                wait_bytes(own.at[0, 0], str_s.at[n % 2, chunk_of(n // 2 - 1)])
            kk = chunk_of(n // 2)
            h = hnear if n % 2 else hfar
            copy_to(own.at[kk, h], end_in.at[kk, h], str_s.at[n % 2, kk], end_r.at[kk, h], at_my_mid).start()

    def pass_end(k):
        @on_mid
        def _():
            kk = chunk_of(k)
            wait_bytes(end_in.at[kk, hfar], end_r.at[kk, hfar])
            copy_to(end_in.at[kk, hfar], far_in.at[kk], str_s.at[1, kk], far_r.at[kk], at_mid).start()

    def pass_mid(k):
        @on_mid
        def _():
            kk = chunk_of(k)
            wait_bytes(mid_in.at[kk], mid_r.at[kk])
            copy_to(mid_in.at[kk], mid_in.at[kk], str_s.at[2, kk], mid_r.at[kk], at_end).start()

    def pass_far(k):
        @on_mid
        def _():
            kk = chunk_of(k)
            wait_bytes(far_in.at[kk], far_r.at[kk])
            copy_to(far_in.at[kk], far_in.at[kk], str_s.at[3, kk], far_r.at[kk], at_end).start()

    send_sums(sums, 0)
    send_mid(0)
    send_end(0)

    za.wait_recv()
    zb.wait_recv()
    low = jnp.full((ROWS, BLK), r, jnp.int32) == 0
    wa = line_f[0:ROWS]
    wb = otherw[...].astype(F32)[0:ROWS]
    west = jnp.concatenate([jnp.where(low, wa, wb), jnp.where(low, wb, wa)], axis=0).astype(BF16)
    south = jnp.where(
        jnp.full((SIDE, BLK), r, jnp.int32) == 0, field[0, 0].astype(F32), others[...].astype(F32)
    ).astype(BF16)

    def place(p, a, b):
        return face_of(a, b, c) if p == 0 else face_of(b, a, c)

    here_on = [(y, x), (x, y)]
    for p in range(2):
        a, b = here_on[p]
        ls = slice(256 * p, 256 * p + 256)
        lines[p, 0] = west[:, ls]
        lines[p, 1] = south[:, ls]
        gathered[p, c, a, 0] = west[:, ls]
        gathered[p, c, a, 1] = south[:, ls]
        for step in range(1, 4):
            n = 1 + 3 * p + step
            copy_to(
                lines.at[p], gathered.at[p, c, a], halo_s.at[n], halo_r.at[n], (s, place(p, (a + step) % 4, b), r)
            ).start()

    send_mid(1)
    pass_mid(0)
    send_end(1)

    wait_sums(sums, 0)
    mean = (sums[0] + sums[1] + sums[2] + sums[3]) * (1.0 / SNAPS)
    sources = [other_mid, other_end, my_end]
    deltas = [weights * (sums[p] * (1.0 / BLK) - mean) for p in sources]

    def pick(matrix, i):
        return jnp.sum(jnp.where(lane == i, matrix, 0.0), axis=1, keepdims=True)

    def inner_anomaly(i, carry):
        w = column(weight_row(i))
        anom[0, i] = (w * (slope[i] - pick(mean, i))).astype(BF16)
        for b in range(3):
            shift[b, i] = jnp.broadcast_to(pick(deltas[b], i), (SIDE, LANE)).astype(BF16)
        return carry

    lax.fori_loop(0, 22, inner_anomaly, 0)
    pass_end(0)
    pass_mid(1)
    send_end(2)

    for p in range(2):
        a, b = here_on[p]
        for step in range(1, 4):
            wait_bytes(lines.at[p], halo_r.at[1 + 3 * p + step])
        copy_to(gathered.at[p, c], gathered.at[p, c], halo_s.at[8 + p], halo_r.at[8 + p], at_core).start()
    send_mid(2)
    pass_far(0)
    send_end(3)

    def request(tile, side_index):
        u = links[2 * tile + side_index]
        turn = links[64 + 2 * tile + side_index]
        return u // 8, (u // 2) % 4, u % 2, turn // 2, turn % 2

    for p in range(2):
        wait_bytes(gathered.at[p, 0], halo_r.at[8 + p])
    for p in range(2):
        a, b = here_on[p]
        for bd in range(4):
            for m in range(2):
                uy, ux, uc, q, odd = request(place(p, a, bd), m)
                chosen[p, bd, m] = gathered[p, uc, uy if p == 0 else ux, q]
        arrived[p, b] = chosen[p, b]
        for step in range(1, 4):
            bd = (b + step) % 4
            n = 9 + 3 * p + step
            to = (s, place(p, a, bd), r)
            copy_to(chosen.at[p, bd, 0], arrived.at[p, b, 0], halo_s.at[n], halo_r.at[n], to).start()

            @pl.when(r == 1)
            def _():
                copy_to(chosen.at[p, bd, 1], arrived.at[p, b, 1], halo_s.at[n + 6], halo_r.at[n + 6], to).start()

    pass_end(1)
    pass_mid(2)
    send_end(4)

    def product(chunk, rows):
        k_size = chunk.shape[0] * chunk.shape[1]
        return lax.dot_general(
            chunk.reshape(k_size, LANE),
            rows.reshape(k_size, BLK),
            (((0,), (0,)), ((), ())),
            preferred_element_type=F32,
        )

    def inner_product(chunk, h):
        return product(chunk[...], anom[0, pl.ds(11 * h, 11)])

    def own_product(kk):
        cols = anom[0, 0:22, :, pl.ds(pl.multiple_of(kk * LANE, LANE), LANE)]
        live = lax.broadcasted_iota(jnp.int32, (22, SIDE, LANE), 1) < SIDE - 1
        cols = jnp.where(live, cols.astype(F32), 0.0).astype(BF16)
        return product(cols, anom[0, 0:22])

    near_inner = pl.ds(11 * hnear, 11)
    level[0] = product(shift[0, near_inner], anom[0, near_inner])
    level[1] = product(shift[1, near_inner], anom[0, near_inner])

    @on_mid
    def _():
        level[2] = product(shift[2], anom[0, 0:22])

    def products(k):
        kk = chunk_of(k)
        acc[0, k] = own_product(kk)

        @on_end
        def _():
            wait_bytes(mid_in.at[kk], mid_r.at[kk])
            wait_bytes(far_in.at[kk], far_r.at[kk])

        acc[1, k] = inner_product(mid_in.at[kk], hnear)
        acc[2, k] = inner_product(far_in.at[kk], hnear)

        @on_mid
        def _():
            wait_bytes(end_in.at[kk, hnear], end_r.at[kk, hnear])
            acc[3, k] = inner_product(end_in.at[kk, 0], 0) + inner_product(end_in.at[kk, 1], 1)

    products(0)

    for p in range(2):
        for step in range(1, 4):
            n = 9 + 3 * p + step
            wait_bytes(arrived.at[0, 0, 0], halo_r.at[n])

            @pl.when(r == 1)
            def _():
                wait_bytes(arrived.at[0, 0, 0], halo_r.at[n + 6])

    row_id = lax.broadcasted_iota(jnp.int32, (SIDE, SIDE), 0)
    col_id = lax.broadcasted_iota(jnp.int32, (SIDE, SIDE), 1)
    for p in range(2):
        ls = slice(256 * p, 256 * p + 256)
        uy, ux, uc, q, odd = request(f, 0)
        cell = row_id[0:32] + 24 * r
        flip = jnp.where(col_id[0:32] == cell + odd * (47 - 2 * cell), 1.0, 0.0).astype(BF16)
        east[:, ls] = jnp.dot(flip, arrived[p, ux if p == 0 else uy, 0], preferred_element_type=F32)

        @pl.when(r == 1)
        def _():
            uy, ux, uc, q, odd = request(f, 1)
            flip = jnp.where(col_id == row_id + odd * (47 - 2 * row_id), 1.0, 0.0).astype(BF16)
            north[:, ls] = jnp.dot(flip, arrived[p, ux if p == 0 else uy, 1], preferred_element_type=F32)

    @pl.when(r == 0)
    def _():
        north[...] = others[...].astype(F32)

    esum = zero
    cells[...] = jnp.zeros_like(cells)
    for h in range(2):
        i = 22 + h
        here = field[0, i].astype(F32)
        above = north[...] if h else field[0, i + 1].astype(F32)
        right = jnp.where(last, east[i : i + 1, :], pltpu.roll(here, SIDE - 1, 0))
        value = steepness(right - here, above - here, column(1.0 / area[0, i : i + 1, :]))
        slope[i] = value
        sv = jnp.sum(value, axis=1, keepdims=True)
        esum = jnp.where(lane == h, sv, esum)
        cells[h, 0:SIDE] = column(weight_row(i)) * (value - sv * (1.0 / BLK))
    ecol = edge_f[...]
    esteep = steepness(
        east[0:ROWS] - ecol, pltpu.roll(ecol, ROWS - 1, 0) - ecol, 1.0 / area[0][:, SIDE - 1 : SIDE]
    )
    slope_e[...] = esteep
    ew = jnp.sqrt(area[0][:, SIDE - 1 : SIDE]) * mask[0][:, SIDE - 1 : SIDE].astype(F32)
    esv = jnp.sum(esteep, axis=1, keepdims=True)
    evalue = ew * (esteep - esv * (1.0 / BLK))
    for h in range(2):
        cells[h, SIDE : SIDE + 11] = evalue[11 * h : 11 * h + 11]
        both = cells[h].astype(BF16)
        for k in range(4):
            edge_own[h, k] = both[:, LANE * k : LANE * k + LANE]

    @on_mid
    def _():
        copy_to(edge_own.at[hfar], edge_mid, edg_s.at[0], edg_r.at[2], at_mid).start()

    @on_end
    def _():
        copy_to(edge_own.at[hfar], edge_end.at[hfar], edg_s.at[0], edg_r.at[hfar], at_my_mid).start()
        copy_to(edge_own.at[hnear], edge_end.at[hnear], edg_s.at[1], edg_r.at[hnear], at_my_mid).start()

    colsum = jnp.concatenate([esv, jnp.zeros((SIDE - ROWS, 1), F32)], axis=0)
    sums_e[s] = jnp.where(lane == 2, colsum, esum)
    send_sums(sums_e, 1)
    send_mid(3)
    pass_far(1)
    send_end(5)
    products(1)

    @on_mid
    def _():
        wait_bytes(edge_end.at[0], edg_r.at[hfar])
        copy_to(edge_end.at[hfar], edge_far, edg_s.at[1], edg_r.at[3], at_mid).start()
        wait_bytes(edge_mid, edg_r.at[2])
        copy_to(edge_mid, edge_mid, edg_s.at[2], edg_r.at[2], at_end).start()

    wait_sums(sums_e, 1)
    emean = (sums_e[0] + sums_e[1] + sums_e[2] + sums_e[3]) * (1.0 / SNAPS)
    evalue = ew * (slope_e[...] - pick(emean, 2)[0:ROWS])
    slope_e[...] = evalue
    for h in range(2):
        i = 22 + h
        w = column(weight_row(i))
        cells[h, 0:SIDE] = w * (slope[i] - pick(emean, h))
        cells[h, SIDE : SIDE + 11] = evalue[11 * h : 11 * h + 11]
        both = cells[h].astype(BF16)
        anom[0, i] = both[0:SIDE]
        edge_rows[h] = both
    pass_end(2)
    pass_mid(3)
    send_end(6)
    shift_e[...] = jnp.zeros_like(shift_e)
    for h in range(2):
        w = column(weight_row(22 + h))
        for b in range(3):
            delta = sums_e[sources[b]] * (1.0 / BLK) - emean
            shift_e[b, h, 0:SIDE] = jnp.broadcast_to(w * pick(delta, h), (SIDE, LANE))
            rim = ew * pick(delta, 2)[0:ROWS]
            shift_e[b, h, SIDE : SIDE + 11] = jnp.broadcast_to(rim[11 * h : 11 * h + 11], (11, LANE))
    near_edge = edge_rows[hnear][None]
    level[0] += product(shift_e[0, hnear].astype(BF16)[None], near_edge)
    level[1] += product(shift_e[1, hnear].astype(BF16)[None], near_edge)

    @on_mid
    def _():
        level[2] += product(shift_e[2].astype(BF16), edge_rows[...])
        wait_bytes(edge_far, edg_r.at[3])
        copy_to(edge_far, edge_far, edg_s.at[3], edg_r.at[3], at_end).start()
        wait_bytes(edge_end.at[0], edg_r.at[hnear])

    @on_end
    def _():
        wait_bytes(edge_mid, edg_r.at[2])
        wait_bytes(edge_far, edg_r.at[3])

    def put_column(i, carry):
        tile = anom[0, i, 32:48].astype(F32)
        at = lax.broadcasted_iota(jnp.int32, (16, BLK), 0) == 15
        anom[0, i, 32:48] = jnp.where(at, slope_e[pl.ds(i, 1), :], tile).astype(BF16)
        return carry

    def plane(mid):
        nb = 4 if mid else 3
        nt = nb - 1

        def emit(k):
            kk = chunk_of(k)
            cols = pl.ds(pl.multiple_of(kk * LANE, LANE), LANE)
            extra = [
                product(edge_rows[:, :, cols], edge_rows[...]),
                product(edge_mid[kk][None], near_edge) + level[0],
                product(edge_far[kk][None], near_edge) + level[1],
            ]
            if mid:
                extra.append(product(edge_end[:, kk], edge_rows[...]) + level[2])
            for b in range(nb):
                pt = acc[b, k] + extra[b]
                p = jnp.transpose(pt).reshape(16, 2, 16, LANE)
                for core in range(2):
                    @pl.when(c == core)
                    def _():
                        keep[k, 16 * b : 16 * b + 16] = p[:, core]
                        give[k, 16 * b : 16 * b + 16] = p[:, 1 - core].astype(BF16)
                if b > 0:
                    o = 16 * (nb + b - 1)
                    pq = pt.reshape(4, 2, 16, BLK)
                    for core in range(2):
                        @pl.when(c == core)
                        def _():
                            for xd in range(4):
                                for l in range(4):
                                    ls = slice(LANE * l, LANE * l + LANE)
                                    keep[k, o + 4 * xd + l] = pq[xd, core, :, ls]
                                    give[k, o + 4 * xd + l] = pq[xd, 1 - core, :, ls].astype(BF16)
            copy_to(
                give.at[k, 0 : 16 * (nb + nt)],
                take.at[k, 0 : 16 * (nb + nt)],
                pair_s.at[k],
                pair_r.at[k],
                at_core,
            ).start()

        def spread(k):
            kk = chunk_of(k)
            wait_bytes(take.at[k, 0 : 16 * (nb + nt)], pair_r.at[k])
            for b in range(nb):
                v = keep[k, 16 * b : 16 * b + 16] + take[k, 16 * b : 16 * b + 16].astype(F32)
                mixed_d[k, :, b] = v.astype(BF16)
            for b in range(nt):
                o = 16 * (nb + b)
                v = keep[k, o : o + 16] + take[k, o : o + 16].astype(F32)
                mixed_t[k, :, 4 * b : 4 * b + 4] = v.astype(BF16).reshape(4, 4, 16, LANE)
            red_d[k, chip, 0:nb] = mixed_d[k, chip, 0:nb]

            def send_direct(step, carry):
                to = (chip + step) % 16
                copy_to(
                    mixed_d.at[k, to, 0:nb],
                    red_d.at[k, chip, 0:nb],
                    dir_s.at[k],
                    dir_r.at[k],
                    (s, 2 * to + c, r),
                ).start()
                return carry

            lax.fori_loop(1, 16, send_direct, 0)

            def send_turned(step, carry):
                xd = (x + step) % 4
                copy_to(
                    mixed_t.at[k, xd, 0 : 4 * nt],
                    red_t.at[chip, 0 : 4 * nt],
                    tra_s.at[k],
                    tra_r.at[k],
                    (s, face_of(kk, xd, c), r),
                ).start()
                return carry

            lax.fori_loop(1, 4, send_turned, 0)

            if k == 0:
                red_t[chip, 0 : 4 * nt] = mixed_t[k, x, 0 : 4 * nt]
            else:
                send_turned(0, 0)

        def gather_step(k):
            wait_bytes(red_d.at[0, 0:15, 0:nb], dir_r.at[k])
            for yi in range(4):
                part = red_d[k, 4 * yi, 0:nb].astype(F32)
                for xi in range(1, 4):
                    part = part + red_d[k, 4 * yi + xi, 0:nb].astype(F32)
                j = (k + yi) % 4
                if k == 0:
                    tot[j, 0:nb] = part
                else:
                    tot[j, 0:nb] += part

        emit(0)
        pass_end(3)
        pass_far(2)
        send_end(7)
        emit(1)
        spread(0)
        products(2)
        pass_far(3)
        emit(2)
        spread(1)
        products(3)
        emit(3)
        spread(2)
        lax.fori_loop(0, 22, put_column, 0)
        spread(3)
        for k in range(4):
            gather_step(k)
        for k in range(4):
            wait_bytes(red_t.at[0 : (3 if k == 0 else 4), 0 : 4 * nt], tra_r.at[k])

        for k in range(4):
            ls = slice(LANE * k, LANE * k + LANE)
            ln = slice(LANE * (k % 2), LANE * (k % 2) + LANE)
            rn = slice(8 * (k // 2), 8 * (k // 2) + 8)

            total = tot[k, 0:nb]
            for q in range(2):
                piece_d[q, :, ls] = total[0, 8 * q : 8 * q + 8]
                for b in range(nt):
                    piece_n[q, b, rn, ln] = total[1 + b, 8 * q : 8 * q + 8]

        def add_turned(i, acc):
            return acc + red_t[i, 0 : 4 * nt].astype(F32)

        total = lax.fori_loop(1, 16, add_turned, red_t[0, 0 : 4 * nt].astype(F32))
        for b in range(nt):
            for q in range(2):
                rows = slice(8 * q, 8 * q + 8)
                parts = [total[4 * b + l, rows] for l in range(4)]
                top = jnp.concatenate(parts[0:2], axis=1)
                bottom = jnp.concatenate(parts[2:4], axis=1)
                piece_t[q, b] = jnp.concatenate([top, bottom], axis=0).astype(BF16)
        for b in range(nt):
            mixed_n[b] = piece_n[1 - r, b].astype(BF16)

        ends = []
        e = copy_to(piece_d.at[1 - r], fin_d, fin_s.at[0], fin_r.at[0], other_row)
        e.start()
        ends.append(e)
        e = copy_to(mixed_n.at[0:nt], fin_n.at[0:nt], fin_s.at[7], fin_r.at[9], other_row)
        e.start()
        ends.append(e)
        others_of = [other_mid, other_end] + ([my_end] if mid else [])
        for b in range(nt):
            for q in range(2):
                e = copy_to(
                    piece_t.at[q, b],
                    fin_t.at[s, r],
                    fin_s.at[1 + 2 * b + q],
                    fin_r.at[1 + 2 * s + r],
                    (others_of[b], f, q),
                )
                e.start()
                ends.append(e)
        wait_bytes(fin_d, fin_r.at[0])
        wait_bytes(fin_n.at[0:nt], fin_r.at[9])
        sources = [other_mid, other_end] + ([] if mid else [my_mid])
        for p in sources:
            for q in range(2):
                wait_bytes(fin_t.at[p, q], fin_r.at[1 + 2 * p + q])

        def put(block, value):
            gram[:, pl.ds(pl.multiple_of(block * BLK, BLK), BLK)] = value * GRAM_SCALE

        def put_folded(block, value):
            put(block, jnp.concatenate([value[0:8], value[8:16]], axis=1))

        def turned(p):
            return fin_t[p, 0].astype(F32) + fin_t[p, 1].astype(F32)

        def straight(b):
            return piece_n[r, b] + fin_n[b].astype(F32)

        put(s, piece_d[r] + fin_d[...])
        put_folded(other_mid, straight(0) + turned(other_mid))
        put_folded(other_end, straight(1) + turned(other_end))
        if mid:
            put_folded(my_end, straight(2))
        else:
            put_folded(my_mid, turned(my_mid))

        for e in ends:
            e.wait_send()
        if not mid:
            wait_bytes(own.at[0, 0], str_s.at[0, chunk_of(3)])
            wait_bytes(own.at[0, 0], str_s.at[1, chunk_of(3)])
        for k in range(4):
            if mid:
                wait_bytes(own.at[0, 0], str_s.at[0, k])
                wait_bytes(own.at[0, 0], str_s.at[1, k])
                wait_bytes(own.at[0, 0], str_s.at[2, k])
                wait_bytes(own.at[0, 0], str_s.at[3, k])
            wait_bytes(edge_own.at[0], edg_s.at[k]) if mid or k < 2 else None
            wait_bytes(give.at[k, 0 : 16 * (nb + nt)], pair_s.at[k])
            wait_bytes(mixed_d.at[0, 0:15, 0:nb], dir_s.at[k])
            wait_bytes(red_t.at[0 : (3 if k == 0 else 4), 0 : 4 * nt], tra_s.at[k])

    @on_mid
    def _():
        plane(True)

    @on_end
    def _():
        plane(False)

    za.wait_send()
    zb.wait_send()
    for p in range(2):
        for step in range(1, 4):
            wait_bytes(lines.at[p], halo_s.at[1 + 3 * p + step])
            wait_bytes(arrived.at[0, 0, 0], halo_s.at[9 + 3 * p + step])

            @pl.when(r == 1)
            def _():
                wait_bytes(arrived.at[0, 0, 0], halo_s.at[15 + 3 * p + step])

        wait_bytes(gathered.at[p, 0], halo_s.at[8 + p])


def per_device(surface_field, ocean_mask, cell_area, tile_links, edge_turns):
    vmem = pl.BlockSpec(memory_space=pltpu.VMEM)
    smem = pl.BlockSpec(memory_space=pltpu.SMEM)
    dma = pltpu.SemaphoreType.DMA
    links = jnp.concatenate([tile_links.reshape(-1), edge_turns.reshape(-1)])
    return pl.pallas_call(
        kernel,
        out_shape=(
            jax.ShapeDtypeStruct((1, ROWS, SIDE, BLK), BF16),
            jax.ShapeDtypeStruct((8, SNAPS), F32),
        ),
        in_specs=[smem, vmem, vmem, vmem],
        out_specs=(vmem, vmem),
        scratch_shapes=[
            pltpu.VMEM((32, BLK), F32),
            pltpu.VMEM((ROWS, BLK), F32),
            pltpu.VMEM((32, BLK), BF16),
            pltpu.VMEM((32, BLK), BF16),
            pltpu.VMEM((SIDE, BLK), BF16),
            pltpu.VMEM((2, 2, SIDE, 256), BF16),
            pltpu.VMEM((2, 2, 4, 2, SIDE, 256), BF16),
            pltpu.VMEM((2, 4, 2, SIDE, 256), BF16),
            pltpu.VMEM((2, 4, 2, SIDE, 256), BF16),
            pltpu.VMEM((32, BLK), F32),
            pltpu.VMEM((SIDE, BLK), F32),
            pltpu.VMEM((ROWS, SIDE, BLK), F32),
            pltpu.VMEM((ROWS, BLK), F32),
            pltpu.VMEM((2, 64, BLK), F32),
            pltpu.VMEM((4, SIDE, LANE), F32),
            pltpu.VMEM((4, SIDE, LANE), F32),
            pltpu.VMEM((3, 22, SIDE, LANE), BF16),
            pltpu.VMEM((3, 2, 64, LANE), F32),
            pltpu.VMEM((3, LANE, BLK), F32),
            pltpu.VMEM((4, 2, 11, SIDE, LANE), BF16),
            pltpu.VMEM((4, 2, 11, SIDE, LANE), BF16),
            pltpu.VMEM((4, 11, SIDE, LANE), BF16),
            pltpu.VMEM((4, 11, SIDE, LANE), BF16),
            pltpu.VMEM((2, 64, BLK), BF16),
            pltpu.VMEM((2, 4, 64, LANE), BF16),
            pltpu.VMEM((2, 4, 64, LANE), BF16),
            pltpu.VMEM((4, 64, LANE), BF16),
            pltpu.VMEM((4, 64, LANE), BF16),
            pltpu.VMEM((4, 4, LANE, BLK), F32),
            pltpu.VMEM((4, 112, 16, LANE), F32),
            pltpu.VMEM((4, 112, 16, LANE), BF16),
            pltpu.VMEM((4, 112, 16, LANE), BF16),
            pltpu.VMEM((4, 16, 4, 16, LANE), BF16),
            pltpu.VMEM((4, 4, 12, 16, LANE), BF16),
            pltpu.VMEM((4, 16, 4, 16, LANE), BF16),
            pltpu.VMEM((16, 12, 16, LANE), BF16),
            pltpu.VMEM((4, 4, 16, LANE), F32),
            pltpu.VMEM((2, 8, BLK), F32),
            pltpu.VMEM((2, 3, 16, 256), F32),
            pltpu.VMEM((2, 3, 16, 256), BF16),
            pltpu.VMEM((3, 16, 256), BF16),
            pltpu.VMEM((8, BLK), F32),
            pltpu.VMEM((3, 16, 256), BF16),
            pltpu.VMEM((4, 2, 16, 256), BF16),
            dma((22,)),
            dma((22,)),
            dma((2, 4)),
            dma((2, 4)),
            dma((4, 4)),
            dma((4, 2)),
            dma((4,)),
            dma((4,)),
            dma((4,)),
            dma((4,)),
            dma((4,)),
            dma((4,)),
            dma((4,)),
            dma((4,)),
            dma((4,)),
            dma((4,)),
            dma((8,)),
            dma((10,)),
        ],
        compiler_params=pltpu.CompilerParams(
            collective_id=0, has_side_effects=True, vmem_limit_bytes=56 * 1024 * 1024
        ),
        name="slope_gram",
    )(links, surface_field, ocean_mask, cell_area)


def solution(mesh):
    placed = (
        P("face", "row", None, "snapshot"),
        P("face", "row", None),
        P("face", "row", None),
        P(),
        P(),
    )
    return jax.shard_map(
        per_device,
        mesh=mesh,
        in_specs=placed,
        out_specs=(P("face", "row", None, "snapshot"), P(("snapshot", "face", "row"), None)),
        check_vma=False,
    )
```

```python
import functools

import jax
import jax.numpy as jnp
from jax import lax
from jax.experimental import pallas as pl
from jax.experimental.pallas import tpu as pltpu
from jax.sharding import PartitionSpec as P

MESH = pl.DeviceIdType.MESH
BF16 = jnp.bfloat16
F32 = jnp.float32
SNAPS = 2048
ROWS = 24
SIDE = 48
BLK = 512
LANE = 128
SHIFTS = (2, 1, 3, 0)
GRAM_SCALE = 1.0 / (32 * 48 * 48)


def face_of(y, x, c):
    return (y * 4 + x) * 2 + c


def copy_to(src, dst, send_sem, recv_sem, device):
    return pltpu.make_async_remote_copy(
        src_ref=src,
        dst_ref=dst,
        send_sem=send_sem,
        recv_sem=recv_sem,
        device_id=device,
        device_id_type=MESH,
    )


def wait_bytes(ref, sem):
    pltpu.make_async_copy(ref, ref, sem).wait()


def kernel(
    links,
    field,
    mask,
    area,
    anom,
    gram,
    line_f,
    edge_f,
    halfw,
    otherw,
    others,
    lines,
    gathered,
    chosen,
    arrived,
    east,
    north,
    slope,
    slope_e,
    cells,
    sums,
    sums_e,
    shift,
    shift_e,
    level,
    own,
    end_in,
    mid_in,
    far_in,
    edge_rows,
    edge_own,
    edge_end,
    edge_mid,
    edge_far,
    acc,
    keep_a,
    give_a,
    take_a,
    mixed_a,
    red_a,
    keep,
    give,
    take,
    mixed_d,
    mixed_t,
    red_d,
    red_t,
    tot,
    piece_d,
    piece_n,
    piece_t,
    mixed_n,
    fin_d,
    fin_n,
    fin_t,
    halo_s,
    halo_r,
    sum_s,
    sum_r,
    str_s,
    end_r,
    mid_r,
    far_r,
    edg_s,
    edg_r,
    pair_s,
    pair_r,
    dir_s,
    dir_r,
    tra_s,
    tra_r,
    fin_s,
    fin_r,
):
    s = lax.axis_index("snapshot")
    f = lax.axis_index("face")
    r = lax.axis_index("row")
    chip = f // 2
    c = f % 2
    y = chip // 4
    x = chip % 4
    side = s // 2
    is_mid = (s == 1) | (s == 2)
    my_mid = 1 + side
    my_end = 3 * side
    other_mid = 2 - side
    other_end = 3 - 3 * side
    hfar = side
    hnear = 1 - side
    at_mid = (other_mid, f, r)
    at_end = (my_end, f, r)
    at_my_mid = (my_mid, f, r)
    at_core = (s, face_of(y, x, 1 - c), r)

    def on_mid(do):
        pl.when(is_mid)(do)

    def on_end(do):
        pl.when(jnp.logical_not(is_mid))(do)

    def chunk_of(k):
        turn = SHIFTS[k]
        return (y + turn + (x % 2) * ((4 - 2 * turn) % 4)) % 4

    barrier = pltpu.get_barrier_semaphore()

    def greet(device):
        pl.semaphore_signal(barrier, inc=1, device_id=device, device_id_type=MESH)

    greet((s, f, 1 - r))
    greet(at_core)

    def greet_chip(step, carry):
        greet((s, 2 * ((chip + step) % 16) + c, r))
        return carry

    lax.fori_loop(1, 16, greet_chip, 0)

    def greet_plane(step, carry):
        greet(((s + step) % 4, f, r))
        greet(((s + step) % 4, f, 1 - r))
        return carry

    lax.fori_loop(1, 4, greet_plane, 0)

    eye = lax.broadcasted_iota(jnp.int32, (SIDE, SIDE), 0) == lax.broadcasted_iota(jnp.int32, (SIDE, SIDE), 1)
    last = lax.broadcasted_iota(jnp.int32, (SIDE, BLK), 0) == SIDE - 1
    inside = lax.broadcasted_iota(jnp.int32, (SIDE, 1), 0) < SIDE - 1
    lane = lax.broadcasted_iota(jnp.int32, (SIDE, LANE), 1)

    def column(row):
        return jnp.sum(jnp.where(eye, row, 0.0), axis=1, keepdims=True)

    def weight_row(i):
        return jnp.sqrt(area[0, pl.ds(i, 1), :]) * mask[0, pl.ds(i, 1), :].astype(F32)

    def steepness(gc, gr, inv):
        return jnp.sqrt(1.0 + (gc * gc + gr * gr) * inv)

    def inner_row(i, carry):
        total, weights = carry
        here = field[0, i].astype(F32)
        above = field[0, i + 1].astype(F32)
        value = steepness(pltpu.roll(here, SIDE - 1, 0) - here, above - here, column(1.0 / area[0, pl.ds(i, 1), :]))
        slope[i] = value
        sv = jnp.sum(value, axis=1, keepdims=True)
        w = jnp.where(inside, column(weight_row(i)), 0.0)
        out = (w * (value - sv * (1.0 / BLK))).astype(BF16)
        half = i // 11
        for k in range(4):
            own[k, half, i - 11 * half] = out[:, LANE * k : LANE * k + LANE]
        return jnp.where(lane == i, sv, total), jnp.where(lane == i, w, weights)

    zero = jnp.zeros((SIDE, LANE), F32)
    total, weights = lax.fori_loop(0, 22, inner_row, (zero, zero))
    sums[s] = total

    line_f[...] = jnp.zeros_like(line_f)
    for i in range(ROWS):
        line_f[i : i + 1, :] = field[0, i, 0:16, :].astype(F32)[0:1]
        edge_f[i : i + 1, :] = field[0, i, 32:48, :].astype(F32)[15:16]
    halfw[...] = line_f[...].astype(BF16)

    pl.semaphore_wait(barrier, 23)

    other_row = (s, f, 1 - r)
    za = copy_to(halfw, otherw, halo_s.at[0], halo_r.at[0], other_row)
    zb = copy_to(field.at[0, 0], others, halo_s.at[1], halo_r.at[1], other_row)
    za.start()
    zb.start()

    def send_sums(ref, n):
        for step in range(1, 4):
            copy_to(ref.at[s], ref.at[s], sum_s.at[n, step], sum_r.at[n, step], ((s + step) % 4, f, r)).start()

    def wait_sums(ref, n):
        for step in range(1, 4):
            wait_bytes(ref.at[0], sum_r.at[n, step])
        for step in range(1, 4):
            wait_bytes(ref.at[0], sum_s.at[n, step])

    def send_mid(k):
        @on_mid
        def _():
            kk = chunk_of(k)
            copy_to(own.at[kk, hfar], mid_in.at[kk], str_s.at[0, kk], mid_r.at[kk], at_mid).start()

    def send_end(k, far):
        @on_end
        def _():
            kk = chunk_of(k)
            h = hfar if far else hnear
            copy_to(
                own.at[kk, h], end_in.at[kk, h], str_s.at[0 if far else 1, kk], end_r.at[kk, h], at_my_mid
            ).start()

    def pass_end(k):
        @on_mid
        def _():
            kk = chunk_of(k)
            wait_bytes(end_in.at[kk, hfar], end_r.at[kk, hfar])
            copy_to(end_in.at[kk, hfar], far_in.at[kk], str_s.at[1, kk], far_r.at[kk], at_mid).start()

    def pass_mid(k):
        @on_mid
        def _():
            kk = chunk_of(k)
            wait_bytes(mid_in.at[kk], mid_r.at[kk])
            copy_to(mid_in.at[kk], mid_in.at[kk], str_s.at[2, kk], mid_r.at[kk], at_end).start()

    def pass_far(k):
        @on_mid
        def _():
            kk = chunk_of(k)
            wait_bytes(far_in.at[kk], far_r.at[kk])
            copy_to(far_in.at[kk], far_in.at[kk], str_s.at[3, kk], far_r.at[kk], at_end).start()

    send_sums(sums, 0)
    for k in range(4):
        send_mid(k)
        send_end(k, True)
    send_end(0, False)
    send_end(1, False)

    za.wait_recv()
    zb.wait_recv()
    low = jnp.full((ROWS, BLK), r, jnp.int32) == 0
    wa = line_f[0:ROWS]
    wb = otherw[...].astype(F32)[0:ROWS]
    west = jnp.concatenate([jnp.where(low, wa, wb), jnp.where(low, wb, wa)], axis=0).astype(BF16)
    south = jnp.where(
        jnp.full((SIDE, BLK), r, jnp.int32) == 0, field[0, 0].astype(F32), others[...].astype(F32)
    ).astype(BF16)

    def place(p, a, b):
        return face_of(a, b, c) if p == 0 else face_of(b, a, c)

    here_on = [(y, x), (x, y)]
    for p in range(2):
        a, b = here_on[p]
        ls = slice(256 * p, 256 * p + 256)
        lines[p, 0] = west[:, ls]
        lines[p, 1] = south[:, ls]
        gathered[p, c, a, 0] = west[:, ls]
        gathered[p, c, a, 1] = south[:, ls]
        for step in range(1, 4):
            n = 1 + 3 * p + step
            copy_to(
                lines.at[p], gathered.at[p, c, a], halo_s.at[n], halo_r.at[n], (s, place(p, (a + step) % 4, b), r)
            ).start()

    pass_mid(0)

    wait_sums(sums, 0)
    mean = (sums[0] + sums[1] + sums[2] + sums[3]) * (1.0 / SNAPS)
    sources = [other_mid, other_end, my_end]
    deltas = [weights * (sums[p] * (1.0 / BLK) - mean) for p in sources]

    def pick(matrix, i):
        return jnp.sum(jnp.where(lane == i, matrix, 0.0), axis=1, keepdims=True)

    def inner_anomaly(i, carry):
        w = column(weight_row(i))
        anom[0, i] = (w * (slope[i] - pick(mean, i))).astype(BF16)
        for b in range(3):
            shift[b, i] = jnp.broadcast_to(pick(deltas[b], i), (SIDE, LANE)).astype(BF16)
        return carry

    lax.fori_loop(0, 22, inner_anomaly, 0)
    pass_end(0)
    pass_mid(1)

    for p in range(2):
        a, b = here_on[p]
        for step in range(1, 4):
            wait_bytes(lines.at[p], halo_r.at[1 + 3 * p + step])
        copy_to(gathered.at[p, c], gathered.at[p, c], halo_s.at[8 + p], halo_r.at[8 + p], at_core).start()
    pass_mid(2)

    def request(tile, side_index):
        u = links[side_index, tile]
        turn = links[2 + side_index, tile]
        return u // 8, (u // 2) % 4, u % 2, turn // 2, turn % 2

    for p in range(2):
        wait_bytes(gathered.at[p, 0], halo_r.at[8 + p])
    for p in range(2):
        a, b = here_on[p]
        for bd in range(4):
            for m in range(2):
                uy, ux, uc, q, odd = request(place(p, a, bd), m)
                chosen[p, bd, m] = gathered[p, uc, uy if p == 0 else ux, q]
        arrived[p, b] = chosen[p, b]
        for step in range(1, 4):
            bd = (b + step) % 4
            n = 9 + 3 * p + step
            to = (s, place(p, a, bd), r)
            copy_to(chosen.at[p, bd, 0], arrived.at[p, b, 0], halo_s.at[n], halo_r.at[n], to).start()

            @pl.when(r == 1)
            def _():
                copy_to(chosen.at[p, bd, 1], arrived.at[p, b, 1], halo_s.at[n + 6], halo_r.at[n + 6], to).start()

    pass_mid(3)

    def product(chunk, rows):
        k_size = chunk.shape[0] * chunk.shape[1]
        return lax.dot_general(
            chunk.reshape(k_size, LANE),
            rows.reshape(k_size, BLK),
            (((0,), (0,)), ((), ())),
            preferred_element_type=F32,
        )

    def inner_product(chunk, h):
        return product(chunk[...], anom[0, pl.ds(11 * h, 11)])

    def own_product(kk):
        cols = anom[0, 0:22, :, pl.ds(pl.multiple_of(kk * LANE, LANE), LANE)]
        live = lax.broadcasted_iota(jnp.int32, (22, SIDE, LANE), 1) < SIDE - 1
        cols = jnp.where(live, cols.astype(F32), 0.0).astype(BF16)
        return product(cols, anom[0, 0:22])

    near_inner = pl.ds(11 * hnear, 11)
    level[0] = product(shift[0, near_inner], anom[0, near_inner])
    level[1] = product(shift[1, near_inner], anom[0, near_inner])

    @on_mid
    def _():
        level[2] = product(shift[2], anom[0, 0:22])

    def early_product(k):
        kk = chunk_of(k)
        acc[0, k] = own_product(kk)
        on_end(lambda: wait_bytes(mid_in.at[kk], mid_r.at[kk]))
        acc[1, k] = inner_product(mid_in.at[kk], hnear)

    def late_product(k):
        kk = chunk_of(k)
        on_end(lambda: wait_bytes(far_in.at[kk], far_r.at[kk]))
        acc[2, k] = inner_product(far_in.at[kk], hnear)

        @on_mid
        def _():
            wait_bytes(end_in.at[kk, hnear], end_r.at[kk, hnear])
            acc[3, k] = inner_product(end_in.at[kk, 0], 0) + inner_product(end_in.at[kk, 1], 1)

    early_product(0)
    early_product(1)

    for p in range(2):
        for step in range(1, 4):
            n = 9 + 3 * p + step
            wait_bytes(arrived.at[0, 0, 0], halo_r.at[n])

            @pl.when(r == 1)
            def _():
                wait_bytes(arrived.at[0, 0, 0], halo_r.at[n + 6])

    row_id = lax.broadcasted_iota(jnp.int32, (SIDE, SIDE), 0)
    col_id = lax.broadcasted_iota(jnp.int32, (SIDE, SIDE), 1)
    for p in range(2):
        ls = slice(256 * p, 256 * p + 256)
        uy, ux, uc, q, odd = request(f, 0)
        cell = row_id[0:32] + 24 * r
        flip = jnp.where(col_id[0:32] == cell + odd * (47 - 2 * cell), 1.0, 0.0).astype(BF16)
        east[:, ls] = jnp.dot(flip, arrived[p, ux if p == 0 else uy, 0], preferred_element_type=F32)

        @pl.when(r == 1)
        def _():
            uy, ux, uc, q, odd = request(f, 1)
            flip = jnp.where(col_id == row_id + odd * (47 - 2 * row_id), 1.0, 0.0).astype(BF16)
            north[:, ls] = jnp.dot(flip, arrived[p, ux if p == 0 else uy, 1], preferred_element_type=F32)

    @pl.when(r == 0)
    def _():
        north[...] = others[...].astype(F32)

    esum = zero
    cells[...] = jnp.zeros_like(cells)
    for h in range(2):
        i = 22 + h
        here = field[0, i].astype(F32)
        above = north[...] if h else field[0, i + 1].astype(F32)
        right = jnp.where(last, east[i : i + 1, :], pltpu.roll(here, SIDE - 1, 0))
        value = steepness(right - here, above - here, column(1.0 / area[0, i : i + 1, :]))
        slope[i] = value
        sv = jnp.sum(value, axis=1, keepdims=True)
        esum = jnp.where(lane == h, sv, esum)
        cells[h, 0:SIDE] = column(weight_row(i)) * (value - sv * (1.0 / BLK))
    ecol = edge_f[...]
    esteep = steepness(
        east[0:ROWS] - ecol, pltpu.roll(ecol, ROWS - 1, 0) - ecol, 1.0 / area[0][:, SIDE - 1 : SIDE]
    )
    slope_e[...] = esteep
    ew = jnp.sqrt(area[0][:, SIDE - 1 : SIDE]) * mask[0][:, SIDE - 1 : SIDE].astype(F32)
    esv = jnp.sum(esteep, axis=1, keepdims=True)
    evalue = ew * (esteep - esv * (1.0 / BLK))
    for h in range(2):
        cells[h, SIDE : SIDE + 11] = evalue[11 * h : 11 * h + 11]
        both = cells[h].astype(BF16)
        for k in range(4):
            edge_own[h, k] = both[:, LANE * k : LANE * k + LANE]

    @on_mid
    def _():
        copy_to(edge_own.at[hfar], edge_mid, edg_s.at[0], edg_r.at[2], at_mid).start()

    @on_end
    def _():
        copy_to(edge_own.at[hfar], edge_end.at[hfar], edg_s.at[0], edg_r.at[hfar], at_my_mid).start()
        copy_to(edge_own.at[hnear], edge_end.at[hnear], edg_s.at[1], edg_r.at[hnear], at_my_mid).start()

    colsum = jnp.concatenate([esv, jnp.zeros((SIDE - ROWS, 1), F32)], axis=0)
    sums_e[s] = jnp.where(lane == 2, colsum, esum)
    send_sums(sums_e, 1)
    send_end(2, False)
    send_end(3, False)
    pass_end(1)
    pass_end(2)
    early_product(2)
    early_product(3)
    pass_far(0)

    @on_mid
    def _():
        wait_bytes(edge_mid, edg_r.at[2])
        copy_to(edge_mid, edge_mid, edg_s.at[2], edg_r.at[2], at_end).start()

    wait_sums(sums_e, 1)
    emean = (sums_e[0] + sums_e[1] + sums_e[2] + sums_e[3]) * (1.0 / SNAPS)
    evalue = ew * (slope_e[...] - pick(emean, 2)[0:ROWS])
    slope_e[...] = evalue
    for h in range(2):
        i = 22 + h
        w = column(weight_row(i))
        cells[h, 0:SIDE] = w * (slope[i] - pick(emean, h))
        cells[h, SIDE : SIDE + 11] = evalue[11 * h : 11 * h + 11]
        both = cells[h].astype(BF16)
        anom[0, i] = both[0:SIDE]
        edge_rows[h] = both
    shift_e[...] = jnp.zeros_like(shift_e)
    for h in range(2):
        w = column(weight_row(22 + h))
        for b in range(3):
            delta = sums_e[sources[b]] * (1.0 / BLK) - emean
            shift_e[b, h, 0:SIDE] = jnp.broadcast_to(w * pick(delta, h), (SIDE, LANE))
            rim = ew * pick(delta, 2)[0:ROWS]
            shift_e[b, h, SIDE : SIDE + 11] = jnp.broadcast_to(rim[11 * h : 11 * h + 11], (11, LANE))
    near_edge = edge_rows[hnear][None]
    level[0] += product(shift_e[0, hnear].astype(BF16)[None], near_edge)
    level[1] += product(shift_e[1, hnear].astype(BF16)[None], near_edge)

    @on_mid
    def _():
        level[2] += product(shift_e[2].astype(BF16), edge_rows[...])

    on_end(lambda: wait_bytes(edge_mid, edg_r.at[2]))

    def put_column(i, carry):
        tile = anom[0, i, 32:48].astype(F32)
        at = lax.broadcasted_iota(jnp.int32, (16, BLK), 0) == 15
        anom[0, i, 32:48] = jnp.where(at, slope_e[pl.ds(i, 1), :], tile).astype(BF16)
        return carry

    def plane(mid):
        nl = 2 if mid else 1
        nt = 1 + nl

        def block_of(b, k):
            kk = chunk_of(k)
            cols = pl.ds(pl.multiple_of(kk * LANE, LANE), LANE)
            if b == 0:
                extra = product(edge_rows[:, :, cols], edge_rows[...])
            elif b == 1:
                extra = product(edge_mid[kk][None], near_edge) + level[0]
            elif b == 2:
                extra = product(edge_far[kk][None], near_edge) + level[1]
            else:
                extra = product(edge_end[:, kk], edge_rows[...]) + level[2]
            return acc[b, k] + extra

        def put_straight(pt, keep_at, give_at, o):
            p = jnp.transpose(pt).reshape(16, 2, 16, LANE)
            for core in range(2):
                @pl.when(c == core)
                def _():
                    keep_at[o : o + 16] = p[:, core]
                    give_at[o : o + 16] = p[:, 1 - core].astype(BF16)

        def put_turned(pt, keep_at, give_at, o):
            pq = pt.reshape(4, 2, 16, BLK)
            for core in range(2):
                @pl.when(c == core)
                def _():
                    for xd in range(4):
                        for l in range(4):
                            ls = slice(LANE * l, LANE * l + LANE)
                            keep_at[o + 4 * xd + l] = pq[xd, core, :, ls]
                            give_at[o + 4 * xd + l] = pq[xd, 1 - core, :, ls].astype(BF16)

        def emit_early():
            for k in range(4):
                put_straight(block_of(0, k), keep_a, give_a, 32 * k)
                pt = block_of(1, k)
                put_straight(pt, keep_a, give_a, 32 * k + 16)
                put_turned(pt, keep_a, give_a, 128 + 16 * k)
            copy_to(give_a, take_a, pair_s.at[4], pair_r.at[4], at_core).start()

        def spread_early():
            wait_bytes(take_a, pair_r.at[4])
            for n in range(8):
                o = 16 * n
                mixed_a[:, n] = (keep_a[o : o + 16] + take_a[o : o + 16].astype(F32)).astype(BF16)
            for k in range(4):
                o = 128 + 16 * k
                v = (keep_a[o : o + 16] + take_a[o : o + 16].astype(F32)).astype(BF16)
                mixed_a[pl.ds(4 * chunk_of(k), 4), 8:12] = v.reshape(4, 4, 16, LANE)
            red_a[chip] = mixed_a[chip]

            def send(step, carry):
                to = (chip + step) % 16
                copy_to(mixed_a.at[to], red_a.at[chip], dir_s.at[4], dir_r.at[4], (s, 2 * to + c, r)).start()
                return carry

            lax.fori_loop(1, 16, send, 0)

        def emit(k):
            for i in range(nl):
                pt = block_of(2 + i, k)
                put_straight(pt, keep.at[k], give.at[k], 16 * i)
                put_turned(pt, keep.at[k], give.at[k], 16 * (nl + i))
            copy_to(
                give.at[k, 0 : 32 * nl], take.at[k, 0 : 32 * nl], pair_s.at[k], pair_r.at[k], at_core
            ).start()

        def spread(k):
            kk = chunk_of(k)
            wait_bytes(take.at[k, 0 : 32 * nl], pair_r.at[k])
            for b in range(nl):
                v = keep[k, 16 * b : 16 * b + 16] + take[k, 16 * b : 16 * b + 16].astype(F32)
                mixed_d[k, :, b] = v.astype(BF16)
                o = 16 * (nl + b)
                v = keep[k, o : o + 16] + take[k, o : o + 16].astype(F32)
                mixed_t[k, :, 4 * b : 4 * b + 4] = v.astype(BF16).reshape(4, 4, 16, LANE)
            red_d[k, chip, 0:nl] = mixed_d[k, chip, 0:nl]

            def send_direct(step, carry):
                to = (chip + step) % 16
                copy_to(
                    mixed_d.at[k, to, 0:nl],
                    red_d.at[k, chip, 0:nl],
                    dir_s.at[k],
                    dir_r.at[k],
                    (s, 2 * to + c, r),
                ).start()
                return carry

            lax.fori_loop(1, 16, send_direct, 0)

            def send_turned(step, carry):
                xd = (x + step) % 4
                copy_to(
                    mixed_t.at[k, xd, 0 : 4 * nl],
                    red_t.at[chip, 0 : 4 * nl],
                    tra_s.at[k],
                    tra_r.at[k],
                    (s, face_of(kk, xd, c), r),
                ).start()
                return carry

            lax.fori_loop(1, 4, send_turned, 0)
            if SHIFTS[k] == 0:
                red_t[chip, 0 : 4 * nl] = mixed_t[k, x, 0 : 4 * nl]
            else:
                send_turned(0, 0)

        def column_of(k, yi, odd):
            return (yi + (4 - SHIFTS[k] if odd else SHIFTS[k])) % 4

        def gather_early():
            wait_bytes(red_a.at[0:15], dir_r.at[4])
            for k in range(4):
                for yi in range(4):
                    for odd in range(2):
                        rows = slice(2 * k, 2 * k + 2)
                        part = red_a[4 * yi + odd, rows].astype(F32) + red_a[4 * yi + 2 + odd, rows].astype(F32)
                        j = column_of(k, yi, odd)
                        if k == 0 and odd == 0:
                            tot[j, 0:2] = part
                        else:
                            tot[j, 0:2] += part

        def gather_step(k):
            wait_bytes(red_d.at[0, 0:15, 0:nl], dir_r.at[k])
            for yi in range(4):
                for odd in range(2):
                    part = red_d[k, 4 * yi + odd, 0:nl].astype(F32) + red_d[k, 4 * yi + 2 + odd, 0:nl].astype(F32)
                    j = column_of(k, yi, odd)
                    if k == 0 and odd == 0:
                        tot[j, 2 : 2 + nl] = part
                    else:
                        tot[j, 2 : 2 + nl] += part

        emit_early()
        if mid:
            wait_bytes(edge_end.at[0], edg_r.at[hfar])
            copy_to(edge_end.at[hfar], edge_far, edg_s.at[1], edg_r.at[3], at_mid).start()
        pass_end(3)
        pass_far(1)
        spread_early()
        late_product(0)
        late_product(1)
        pass_far(2)
        wait_bytes(edge_far, edg_r.at[3])
        if mid:
            copy_to(edge_far, edge_far, edg_s.at[3], edg_r.at[3], at_end).start()
            wait_bytes(edge_end.at[0], edg_r.at[hnear])
        emit(0)
        emit(1)
        spread(0)
        pass_far(3)
        spread(1)
        late_product(2)
        emit(2)
        late_product(3)
        emit(3)
        spread(2)
        lax.fori_loop(0, 22, put_column, 0)
        spread(3)
        gather_early()
        for k in range(4):
            gather_step(k)
        for k in range(4):
            wait_bytes(red_t.at[0 : (4 if SHIFTS[k] else 3), 0 : 4 * nl], tra_r.at[k])

        for k in range(4):
            ls = slice(LANE * k, LANE * k + LANE)
            ln = slice(LANE * (k % 2), LANE * (k % 2) + LANE)
            rn = slice(8 * (k // 2), 8 * (k // 2) + 8)

            total = tot[k, 0 : 1 + nt]
            for q in range(2):
                piece_d[q, :, ls] = total[0, 8 * q : 8 * q + 8]
                for b in range(nt):
                    piece_n[q, b, rn, ln] = total[1 + b, 8 * q : 8 * q + 8]

        def add_early(i, acc):
            return acc + red_a[i, 8:12].astype(F32)

        def add_turned(i, acc):
            return acc + red_t[i, 0 : 4 * nl].astype(F32)

        first_sum = lax.fori_loop(1, 16, add_early, red_a[0, 8:12].astype(F32))
        rest_sum = lax.fori_loop(1, 16, add_turned, red_t[0, 0 : 4 * nl].astype(F32))
        total = jnp.concatenate([first_sum, rest_sum], axis=0)
        for b in range(nt):
            for q in range(2):
                rows = slice(8 * q, 8 * q + 8)
                parts = [total[4 * b + l, rows] for l in range(4)]
                top = jnp.concatenate(parts[0:2], axis=1)
                bottom = jnp.concatenate(parts[2:4], axis=1)
                piece_t[q, b] = jnp.concatenate([top, bottom], axis=0).astype(BF16)
        for b in range(nt):
            mixed_n[b] = piece_n[1 - r, b].astype(BF16)

        ends = []
        e = copy_to(piece_d.at[1 - r], fin_d, fin_s.at[0], fin_r.at[0], other_row)
        e.start()
        ends.append(e)
        e = copy_to(mixed_n.at[0:nt], fin_n.at[0:nt], fin_s.at[7], fin_r.at[9], other_row)
        e.start()
        ends.append(e)
        others_of = [other_mid, other_end] + ([my_end] if mid else [])
        for b in range(nt):
            for q in range(2):
                e = copy_to(
                    piece_t.at[q, b],
                    fin_t.at[s, r],
                    fin_s.at[1 + 2 * b + q],
                    fin_r.at[1 + 2 * s + r],
                    (others_of[b], f, q),
                )
                e.start()
                ends.append(e)
        wait_bytes(fin_d, fin_r.at[0])
        wait_bytes(fin_n.at[0:nt], fin_r.at[9])
        sources = [other_mid, other_end] + ([] if mid else [my_mid])
        for p in sources:
            for q in range(2):
                wait_bytes(fin_t.at[p, q], fin_r.at[1 + 2 * p + q])

        def put(block, value):
            gram[:, pl.ds(pl.multiple_of(block * BLK, BLK), BLK)] = value * GRAM_SCALE

        def put_folded(block, value):
            put(block, jnp.concatenate([value[0:8], value[8:16]], axis=1))

        def turned(p):
            return fin_t[p, 0].astype(F32) + fin_t[p, 1].astype(F32)

        def straight(b):
            return piece_n[r, b] + fin_n[b].astype(F32)

        put(s, piece_d[r] + fin_d[...])
        put_folded(other_mid, straight(0) + turned(other_mid))
        put_folded(other_end, straight(1) + turned(other_end))
        if mid:
            put_folded(my_end, straight(2))
        else:
            put_folded(my_mid, turned(my_mid))

        for e in ends:
            e.wait_send()
        for k in range(4):
            wait_bytes(own.at[0, 0], str_s.at[0, k])
            wait_bytes(own.at[0, 0], str_s.at[1, k])
            if mid:
                wait_bytes(own.at[0, 0], str_s.at[2, k])
                wait_bytes(own.at[0, 0], str_s.at[3, k])
            wait_bytes(edge_own.at[0], edg_s.at[k]) if mid or k < 2 else None
            wait_bytes(give.at[k, 0 : 32 * nl], pair_s.at[k])
            wait_bytes(mixed_d.at[0, 0:15, 0:nl], dir_s.at[k])
            wait_bytes(red_t.at[0 : (4 if SHIFTS[k] else 3), 0 : 4 * nl], tra_s.at[k])
        wait_bytes(give_a, pair_s.at[4])
        wait_bytes(mixed_a.at[0:15], dir_s.at[4])

    @on_mid
    def _():
        plane(True)

    @on_end
    def _():
        plane(False)

    za.wait_send()
    zb.wait_send()
    for p in range(2):
        for step in range(1, 4):
            wait_bytes(lines.at[p], halo_s.at[1 + 3 * p + step])
            wait_bytes(arrived.at[0, 0, 0], halo_s.at[9 + 3 * p + step])

            @pl.when(r == 1)
            def _():
                wait_bytes(arrived.at[0, 0, 0], halo_s.at[15 + 3 * p + step])

        wait_bytes(gathered.at[p, 0], halo_s.at[8 + p])


def per_device(surface_field, ocean_mask, cell_area, tile_links, edge_turns):
    vmem = pl.BlockSpec(memory_space=pltpu.VMEM)
    smem = pl.BlockSpec(memory_space=pltpu.SMEM)
    dma = pltpu.SemaphoreType.DMA
    links = jnp.concatenate([tile_links.T, edge_turns.T], axis=0)
    return pl.pallas_call(
        kernel,
        out_shape=(
            jax.ShapeDtypeStruct((1, ROWS, SIDE, BLK), BF16),
            jax.ShapeDtypeStruct((8, SNAPS), F32),
        ),
        in_specs=[smem, vmem, vmem, vmem],
        out_specs=(vmem, vmem),
        scratch_shapes=[
            pltpu.VMEM((32, BLK), F32),
            pltpu.VMEM((ROWS, BLK), F32),
            pltpu.VMEM((32, BLK), BF16),
            pltpu.VMEM((32, BLK), BF16),
            pltpu.VMEM((SIDE, BLK), BF16),
            pltpu.VMEM((2, 2, SIDE, 256), BF16),
            pltpu.VMEM((2, 2, 4, 2, SIDE, 256), BF16),
            pltpu.VMEM((2, 4, 2, SIDE, 256), BF16),
            pltpu.VMEM((2, 4, 2, SIDE, 256), BF16),
            pltpu.VMEM((32, BLK), F32),
            pltpu.VMEM((SIDE, BLK), F32),
            pltpu.VMEM((ROWS, SIDE, BLK), F32),
            pltpu.VMEM((ROWS, BLK), F32),
            pltpu.VMEM((2, 64, BLK), F32),
            pltpu.VMEM((4, SIDE, LANE), F32),
            pltpu.VMEM((4, SIDE, LANE), F32),
            pltpu.VMEM((3, 22, SIDE, LANE), BF16),
            pltpu.VMEM((3, 2, 64, LANE), F32),
            pltpu.VMEM((3, LANE, BLK), F32),
            pltpu.VMEM((4, 2, 11, SIDE, LANE), BF16),
            pltpu.VMEM((4, 2, 11, SIDE, LANE), BF16),
            pltpu.VMEM((4, 11, SIDE, LANE), BF16),
            pltpu.VMEM((4, 11, SIDE, LANE), BF16),
            pltpu.VMEM((2, 64, BLK), BF16),
            pltpu.VMEM((2, 4, 64, LANE), BF16),
            pltpu.VMEM((2, 4, 64, LANE), BF16),
            pltpu.VMEM((4, 64, LANE), BF16),
            pltpu.VMEM((4, 64, LANE), BF16),
            pltpu.VMEM((4, 4, LANE, BLK), F32),
            pltpu.VMEM((192, 16, LANE), F32),
            pltpu.VMEM((192, 16, LANE), BF16),
            pltpu.VMEM((192, 16, LANE), BF16),
            pltpu.VMEM((16, 12, 16, LANE), BF16),
            pltpu.VMEM((16, 12, 16, LANE), BF16),
            pltpu.VMEM((4, 64, 16, LANE), F32),
            pltpu.VMEM((4, 64, 16, LANE), BF16),
            pltpu.VMEM((4, 64, 16, LANE), BF16),
            pltpu.VMEM((4, 16, 2, 16, LANE), BF16),
            pltpu.VMEM((4, 4, 8, 16, LANE), BF16),
            pltpu.VMEM((4, 16, 2, 16, LANE), BF16),
            pltpu.VMEM((16, 8, 16, LANE), BF16),
            pltpu.VMEM((4, 4, 16, LANE), F32),
            pltpu.VMEM((2, 8, BLK), F32),
            pltpu.VMEM((2, 3, 16, 256), F32),
            pltpu.VMEM((2, 3, 16, 256), BF16),
            pltpu.VMEM((3, 16, 256), BF16),
            pltpu.VMEM((8, BLK), F32),
            pltpu.VMEM((3, 16, 256), BF16),
            pltpu.VMEM((4, 2, 16, 256), BF16),
            dma((22,)),
            dma((22,)),
            dma((2, 4)),
            dma((2, 4)),
            dma((4, 4)),
            dma((4, 2)),
            dma((4,)),
            dma((4,)),
            dma((4,)),
            dma((4,)),
            dma((5,)),
            dma((5,)),
            dma((5,)),
            dma((5,)),
            dma((4,)),
            dma((4,)),
            dma((8,)),
            dma((10,)),
        ],
        compiler_params=pltpu.CompilerParams(
            collective_id=0, has_side_effects=True, vmem_limit_bytes=56 * 1024 * 1024
        ),
        name="slope_gram",
    )(links, surface_field, ocean_mask, cell_area)


def solution(mesh):
    placed = (
        P("face", "row", None, "snapshot"),
        P("face", "row", None),
        P("face", "row", None),
        P(),
        P(),
    )
    return jax.shard_map(
        per_device,
        mesh=mesh,
        in_specs=placed,
        out_specs=(P("face", "row", None, "snapshot"), P(("snapshot", "face", "row"), None)),
        check_vma=False,
    )
```

```python
import functools

import jax
import jax.numpy as jnp
from jax import lax
from jax.experimental import pallas as pl
from jax.experimental.pallas import tpu as pltpu
from jax.sharding import PartitionSpec as P

MESH = pl.DeviceIdType.MESH
BF16 = jnp.bfloat16
F32 = jnp.float32
SNAPS = 2048
ROWS = 24
SIDE = 48
BLK = 512
LANE = 128
SHIFTS = (2, 1, 3, 0)
GRAM_SCALE = 1.0 / (32 * 48 * 48)


def face_of(y, x, c):
    return (y * 4 + x) * 2 + c


def copy_to(src, dst, send_sem, recv_sem, device):
    return pltpu.make_async_remote_copy(
        src_ref=src,
        dst_ref=dst,
        send_sem=send_sem,
        recv_sem=recv_sem,
        device_id=device,
        device_id_type=MESH,
    )


def wait_bytes(ref, sem):
    pltpu.make_async_copy(ref, ref, sem).wait()


def kernel(
    links,
    field,
    mask,
    area,
    anom,
    gram,
    line_f,
    edge_f,
    halfw,
    otherw,
    others,
    lines,
    gathered,
    chosen,
    arrived,
    east,
    north,
    slope,
    slope_e,
    cells,
    sums,
    sums_e,
    shift,
    shift_e,
    level,
    own,
    end_in,
    mid_in,
    far_in,
    edge_rows,
    edge_own,
    edge_end,
    edge_mid,
    edge_far,
    acc,
    keep_a,
    give_a,
    take_a,
    mixed_a,
    red_a,
    keep,
    give,
    take,
    mixed_d,
    mixed_t,
    red_d,
    red_t,
    tot,
    piece_d,
    piece_n,
    piece_t,
    mixed_n,
    fin_d,
    fin_n,
    fin_t,
    halo_s,
    halo_r,
    sum_s,
    sum_r,
    str_s,
    end_r,
    mid_r,
    far_r,
    edg_s,
    edg_r,
    pair_s,
    pair_r,
    dir_s,
    dir_r,
    tra_s,
    tra_r,
    fin_s,
    fin_r,
):
    s = lax.axis_index("snapshot")
    f = lax.axis_index("face")
    r = lax.axis_index("row")
    chip = f // 2
    c = f % 2
    y = chip // 4
    x = chip % 4
    side = s // 2
    is_mid = (s == 1) | (s == 2)
    my_mid = 1 + side
    my_end = 3 * side
    other_mid = 2 - side
    other_end = 3 - 3 * side
    hfar = side
    hnear = 1 - side
    at_mid = (other_mid, f, r)
    at_end = (my_end, f, r)
    at_my_mid = (my_mid, f, r)
    at_core = (s, face_of(y, x, 1 - c), r)

    def on_mid(do):
        pl.when(is_mid)(do)

    def on_end(do):
        pl.when(jnp.logical_not(is_mid))(do)

    def chunk_of(k):
        turn = SHIFTS[k]
        return (y + turn + (x % 2) * ((4 - 2 * turn) % 4)) % 4

    barrier = pltpu.get_barrier_semaphore()

    def greet(device):
        pl.semaphore_signal(barrier, inc=1, device_id=device, device_id_type=MESH)

    greet((s, f, 1 - r))
    greet(at_core)

    def greet_chip(step, carry):
        greet((s, 2 * ((chip + step) % 16) + c, r))
        return carry

    lax.fori_loop(1, 16, greet_chip, 0)

    def greet_plane(step, carry):
        greet(((s + step) % 4, f, r))
        greet(((s + step) % 4, f, 1 - r))
        return carry

    lax.fori_loop(1, 4, greet_plane, 0)

    eye = lax.broadcasted_iota(jnp.int32, (SIDE, SIDE), 0) == lax.broadcasted_iota(jnp.int32, (SIDE, SIDE), 1)
    last = lax.broadcasted_iota(jnp.int32, (SIDE, BLK), 0) == SIDE - 1
    inside = lax.broadcasted_iota(jnp.int32, (SIDE, 1), 0) < SIDE - 1
    lane = lax.broadcasted_iota(jnp.int32, (SIDE, LANE), 1)

    def column(row):
        return jnp.sum(jnp.where(eye, row, 0.0), axis=1, keepdims=True)

    def weight_row(i):
        return jnp.sqrt(area[0, pl.ds(i, 1), :]) * mask[0, pl.ds(i, 1), :].astype(F32)

    def steepness(gc, gr, inv):
        return jnp.sqrt(1.0 + (gc * gc + gr * gr) * inv)

    def inner_row(i, carry):
        total, weights = carry
        here = field[0, i].astype(F32)
        above = field[0, i + 1].astype(F32)
        value = steepness(pltpu.roll(here, SIDE - 1, 0) - here, above - here, column(1.0 / area[0, pl.ds(i, 1), :]))
        slope[i] = value
        sv = jnp.sum(value, axis=1, keepdims=True)
        w = jnp.where(inside, column(weight_row(i)), 0.0)
        out = (w * (value - sv * (1.0 / BLK))).astype(BF16)
        half = i // 11
        for k in range(4):
            own[k, half, i - 11 * half] = out[:, LANE * k : LANE * k + LANE]
        return jnp.where(lane == i, sv, total), jnp.where(lane == i, w, weights)

    zero = jnp.zeros((SIDE, LANE), F32)
    total, weights = lax.fori_loop(0, 22, inner_row, (zero, zero))
    sums[s] = total

    line_f[...] = jnp.zeros_like(line_f)
    for i in range(ROWS):
        line_f[i : i + 1, :] = field[0, i, 0:16, :].astype(F32)[0:1]
        edge_f[i : i + 1, :] = field[0, i, 32:48, :].astype(F32)[15:16]
    halfw[...] = line_f[...].astype(BF16)

    pl.semaphore_wait(barrier, 23)

    other_row = (s, f, 1 - r)
    za = copy_to(halfw, otherw, halo_s.at[0], halo_r.at[0], other_row)
    zb = copy_to(field.at[0, 0], others, halo_s.at[1], halo_r.at[1], other_row)
    za.start()
    zb.start()

    def send_sums(ref, n):
        for step in range(1, 4):
            copy_to(ref.at[s], ref.at[s], sum_s.at[n, step], sum_r.at[n, step], ((s + step) % 4, f, r)).start()

    def wait_sums(ref, n):
        for step in range(1, 4):
            wait_bytes(ref.at[0], sum_r.at[n, step])
        for step in range(1, 4):
            wait_bytes(ref.at[0], sum_s.at[n, step])

    def send_mid(k):
        @on_mid
        def _():
            kk = chunk_of(k)
            copy_to(own.at[kk, hfar], mid_in.at[kk], str_s.at[0, kk], mid_r.at[kk], at_mid).start()

    def send_end(k, far):
        @on_end
        def _():
            kk = chunk_of(k)
            h = hfar if far else hnear
            copy_to(
                own.at[kk, h], end_in.at[kk, h], str_s.at[0 if far else 1, kk], end_r.at[kk, h], at_my_mid
            ).start()

    def pass_end(k):
        @on_mid
        def _():
            kk = chunk_of(k)
            wait_bytes(end_in.at[kk, hfar], end_r.at[kk, hfar])
            copy_to(end_in.at[kk, hfar], far_in.at[kk], str_s.at[1, kk], far_r.at[kk], at_mid).start()

    def pass_mid(k):
        @on_mid
        def _():
            kk = chunk_of(k)
            wait_bytes(mid_in.at[kk], mid_r.at[kk])
            copy_to(mid_in.at[kk], mid_in.at[kk], str_s.at[2, kk], mid_r.at[kk], at_end).start()

    def pass_far(k):
        @on_mid
        def _():
            kk = chunk_of(k)
            wait_bytes(far_in.at[kk], far_r.at[kk])
            copy_to(far_in.at[kk], far_in.at[kk], str_s.at[3, kk], far_r.at[kk], at_end).start()

    send_sums(sums, 0)
    for k in range(4):
        send_mid(k)
        send_end(k, True)
    send_end(0, False)
    send_end(1, False)

    za.wait_recv()
    zb.wait_recv()
    low = jnp.full((ROWS, BLK), r, jnp.int32) == 0
    wa = line_f[0:ROWS]
    wb = otherw[...].astype(F32)[0:ROWS]
    west = jnp.concatenate([jnp.where(low, wa, wb), jnp.where(low, wb, wa)], axis=0).astype(BF16)
    south = jnp.where(
        jnp.full((SIDE, BLK), r, jnp.int32) == 0, field[0, 0].astype(F32), others[...].astype(F32)
    ).astype(BF16)

    def place(p, a, b):
        return face_of(a, b, c) if p == 0 else face_of(b, a, c)

    here_on = [(y, x), (x, y)]
    for p in range(2):
        a, b = here_on[p]
        ls = slice(256 * p, 256 * p + 256)
        lines[p, 0] = west[:, ls]
        lines[p, 1] = south[:, ls]
        gathered[p, c, a, 0] = west[:, ls]
        gathered[p, c, a, 1] = south[:, ls]
        for step in range(1, 4):
            n = 1 + 3 * p + step
            copy_to(
                lines.at[p], gathered.at[p, c, a], halo_s.at[n], halo_r.at[n], (s, place(p, (a + step) % 4, b), r)
            ).start()

    pass_mid(0)

    wait_sums(sums, 0)
    mean = (sums[0] + sums[1] + sums[2] + sums[3]) * (1.0 / SNAPS)
    sources = [other_mid, other_end, my_end]
    deltas = [weights * (sums[p] * (1.0 / BLK) - mean) for p in sources]

    def pick(matrix, i):
        return jnp.sum(jnp.where(lane == i, matrix, 0.0), axis=1, keepdims=True)

    def inner_anomaly(i, carry):
        w = column(weight_row(i))
        anom[0, i] = (w * (slope[i] - pick(mean, i))).astype(BF16)
        for b in range(3):
            shift[b, i] = jnp.broadcast_to(pick(deltas[b], i), (SIDE, LANE)).astype(BF16)
        return carry

    lax.fori_loop(0, 22, inner_anomaly, 0)
    pass_end(0)
    pass_mid(1)

    for p in range(2):
        a, b = here_on[p]
        for step in range(1, 4):
            wait_bytes(lines.at[p], halo_r.at[1 + 3 * p + step])
        copy_to(gathered.at[p, c], gathered.at[p, c], halo_s.at[8 + p], halo_r.at[8 + p], at_core).start()
    pass_mid(2)

    def request(tile, side_index):
        u = links[side_index, tile]
        turn = links[2 + side_index, tile]
        return u // 8, (u // 2) % 4, u % 2, turn // 2, turn % 2

    for p in range(2):
        wait_bytes(gathered.at[p, 0], halo_r.at[8 + p])
    for p in range(2):
        a, b = here_on[p]
        for bd in range(4):
            for m in range(2):
                uy, ux, uc, q, odd = request(place(p, a, bd), m)
                chosen[p, bd, m] = gathered[p, uc, uy if p == 0 else ux, q]
        arrived[p, b] = chosen[p, b]
        for step in range(1, 4):
            bd = (b + step) % 4
            n = 9 + 3 * p + step
            to = (s, place(p, a, bd), r)
            copy_to(chosen.at[p, bd, 0], arrived.at[p, b, 0], halo_s.at[n], halo_r.at[n], to).start()

            @pl.when(r == 1)
            def _():
                copy_to(chosen.at[p, bd, 1], arrived.at[p, b, 1], halo_s.at[n + 6], halo_r.at[n + 6], to).start()

    pass_mid(3)

    def product(chunk, rows):
        k_size = chunk.shape[0] * chunk.shape[1]
        return lax.dot_general(
            chunk.reshape(k_size, LANE),
            rows.reshape(k_size, BLK),
            (((0,), (0,)), ((), ())),
            preferred_element_type=F32,
        )

    def inner_product(chunk, h):
        return product(chunk[...], anom[0, pl.ds(11 * h, 11)])

    def own_product(kk):
        cols = anom[0, 0:22, :, pl.ds(pl.multiple_of(kk * LANE, LANE), LANE)]
        live = lax.broadcasted_iota(jnp.int32, (22, SIDE, LANE), 1) < SIDE - 1
        cols = jnp.where(live, cols.astype(F32), 0.0).astype(BF16)
        return product(cols, anom[0, 0:22])

    near_inner = pl.ds(11 * hnear, 11)
    level[0] = product(shift[0, near_inner], anom[0, near_inner])
    level[1] = product(shift[1, near_inner], anom[0, near_inner])

    @on_mid
    def _():
        level[2] = product(shift[2], anom[0, 0:22])

    def early_product(k):
        kk = chunk_of(k)
        acc[0, k] = own_product(kk)
        on_end(lambda: wait_bytes(mid_in.at[kk], mid_r.at[kk]))
        acc[1, k] = inner_product(mid_in.at[kk], hnear)

    def late_product(k):
        kk = chunk_of(k)
        on_end(lambda: wait_bytes(far_in.at[kk], far_r.at[kk]))
        acc[2, k] = inner_product(far_in.at[kk], hnear)

        @on_mid
        def _():
            wait_bytes(end_in.at[kk, hnear], end_r.at[kk, hnear])
            acc[3, k] = inner_product(end_in.at[kk, 0], 0) + inner_product(end_in.at[kk, 1], 1)

    early_product(0)
    early_product(1)

    for p in range(2):
        for step in range(1, 4):
            n = 9 + 3 * p + step
            wait_bytes(arrived.at[0, 0, 0], halo_r.at[n])

            @pl.when(r == 1)
            def _():
                wait_bytes(arrived.at[0, 0, 0], halo_r.at[n + 6])

    row_id = lax.broadcasted_iota(jnp.int32, (SIDE, SIDE), 0)
    col_id = lax.broadcasted_iota(jnp.int32, (SIDE, SIDE), 1)
    for p in range(2):
        ls = slice(256 * p, 256 * p + 256)
        uy, ux, uc, q, odd = request(f, 0)
        cell = row_id[0:32] + 24 * r
        flip = jnp.where(col_id[0:32] == cell + odd * (47 - 2 * cell), 1.0, 0.0).astype(BF16)
        east[:, ls] = jnp.dot(flip, arrived[p, ux if p == 0 else uy, 0], preferred_element_type=F32)

        @pl.when(r == 1)
        def _():
            uy, ux, uc, q, odd = request(f, 1)
            flip = jnp.where(col_id == row_id + odd * (47 - 2 * row_id), 1.0, 0.0).astype(BF16)
            north[:, ls] = jnp.dot(flip, arrived[p, ux if p == 0 else uy, 1], preferred_element_type=F32)

    @pl.when(r == 0)
    def _():
        north[...] = others[...].astype(F32)

    esum = zero
    cells[...] = jnp.zeros_like(cells)
    for h in range(2):
        i = 22 + h
        here = field[0, i].astype(F32)
        above = north[...] if h else field[0, i + 1].astype(F32)
        right = jnp.where(last, east[i : i + 1, :], pltpu.roll(here, SIDE - 1, 0))
        value = steepness(right - here, above - here, column(1.0 / area[0, i : i + 1, :]))
        slope[i] = value
        sv = jnp.sum(value, axis=1, keepdims=True)
        esum = jnp.where(lane == h, sv, esum)
        cells[h, 0:SIDE] = column(weight_row(i)) * (value - sv * (1.0 / BLK))
    ecol = edge_f[...]
    esteep = steepness(
        east[0:ROWS] - ecol, pltpu.roll(ecol, ROWS - 1, 0) - ecol, 1.0 / area[0][:, SIDE - 1 : SIDE]
    )
    slope_e[...] = esteep
    ew = jnp.sqrt(area[0][:, SIDE - 1 : SIDE]) * mask[0][:, SIDE - 1 : SIDE].astype(F32)
    esv = jnp.sum(esteep, axis=1, keepdims=True)
    evalue = ew * (esteep - esv * (1.0 / BLK))
    for h in range(2):
        cells[h, SIDE : SIDE + 11] = evalue[11 * h : 11 * h + 11]
        both = cells[h].astype(BF16)
        for k in range(4):
            edge_own[h, k] = both[:, LANE * k : LANE * k + LANE]

    @on_mid
    def _():
        copy_to(edge_own.at[hfar], edge_mid, edg_s.at[0], edg_r.at[2], at_mid).start()

    @on_end
    def _():
        copy_to(edge_own.at[hfar], edge_end.at[hfar], edg_s.at[0], edg_r.at[hfar], at_my_mid).start()
        copy_to(edge_own.at[hnear], edge_end.at[hnear], edg_s.at[1], edg_r.at[hnear], at_my_mid).start()

    colsum = jnp.concatenate([esv, jnp.zeros((SIDE - ROWS, 1), F32)], axis=0)
    sums_e[s] = jnp.where(lane == 2, colsum, esum)
    send_sums(sums_e, 1)
    send_end(2, False)
    send_end(3, False)
    pass_end(1)
    pass_end(2)
    early_product(2)
    early_product(3)
    pass_far(0)

    @on_mid
    def _():
        wait_bytes(edge_mid, edg_r.at[2])
        copy_to(edge_mid, edge_mid, edg_s.at[2], edg_r.at[2], at_end).start()

    wait_sums(sums_e, 1)
    emean = (sums_e[0] + sums_e[1] + sums_e[2] + sums_e[3]) * (1.0 / SNAPS)
    evalue = ew * (slope_e[...] - pick(emean, 2)[0:ROWS])
    slope_e[...] = evalue
    for h in range(2):
        i = 22 + h
        w = column(weight_row(i))
        cells[h, 0:SIDE] = w * (slope[i] - pick(emean, h))
        cells[h, SIDE : SIDE + 11] = evalue[11 * h : 11 * h + 11]
        both = cells[h].astype(BF16)
        anom[0, i] = both[0:SIDE]
        edge_rows[h] = both
    shift_e[...] = jnp.zeros_like(shift_e)
    for h in range(2):
        w = column(weight_row(22 + h))
        for b in range(3):
            delta = sums_e[sources[b]] * (1.0 / BLK) - emean
            shift_e[b, h, 0:SIDE] = jnp.broadcast_to(w * pick(delta, h), (SIDE, LANE))
            rim = ew * pick(delta, 2)[0:ROWS]
            shift_e[b, h, SIDE : SIDE + 11] = jnp.broadcast_to(rim[11 * h : 11 * h + 11], (11, LANE))
    near_edge = edge_rows[hnear][None]
    level[0] += product(shift_e[0, hnear].astype(BF16)[None], near_edge)
    level[1] += product(shift_e[1, hnear].astype(BF16)[None], near_edge)

    @on_mid
    def _():
        level[2] += product(shift_e[2].astype(BF16), edge_rows[...])

    on_end(lambda: wait_bytes(edge_mid, edg_r.at[2]))

    def put_column(i, carry):
        tile = anom[0, i, 32:48].astype(F32)
        at = lax.broadcasted_iota(jnp.int32, (16, BLK), 0) == 15
        anom[0, i, 32:48] = jnp.where(at, slope_e[pl.ds(i, 1), :], tile).astype(BF16)
        return carry

    def plane(mid):
        nl = 2 if mid else 1
        nt = 1 + nl

        def block_of(b, k):
            kk = chunk_of(k)
            cols = pl.ds(pl.multiple_of(kk * LANE, LANE), LANE)
            if b == 0:
                extra = product(edge_rows[:, :, cols], edge_rows[...])
            elif b == 1:
                extra = product(edge_mid[kk][None], near_edge) + level[0]
            elif b == 2:
                extra = product(edge_far[kk][None], near_edge) + level[1]
            else:
                extra = product(edge_end[:, kk], edge_rows[...]) + level[2]
            return acc[b, k] + extra

        def put_straight(pt, keep_at, give_at, o):
            p = jnp.transpose(pt).reshape(16, 2, 16, LANE)
            for core in range(2):
                @pl.when(c == core)
                def _():
                    keep_at[o : o + 16] = p[:, core]
                    give_at[o : o + 16] = p[:, 1 - core].astype(BF16)

        def put_turned(pt, keep_at, give_at, o):
            pq = pt.reshape(4, 2, 16, BLK)
            for core in range(2):
                @pl.when(c == core)
                def _():
                    for xd in range(4):
                        for l in range(4):
                            ls = slice(LANE * l, LANE * l + LANE)
                            keep_at[o + 4 * xd + l] = pq[xd, core, :, ls]
                            give_at[o + 4 * xd + l] = pq[xd, 1 - core, :, ls].astype(BF16)

        def emit_early():
            for k in range(4):
                put_straight(block_of(0, k), keep_a, give_a, 32 * k)
                pt = block_of(1, k)
                put_straight(pt, keep_a, give_a, 32 * k + 16)
                put_turned(pt, keep_a, give_a, 128 + 16 * k)
            copy_to(give_a, take_a, pair_s.at[4], pair_r.at[4], at_core).start()

        def spread_early():
            wait_bytes(take_a, pair_r.at[4])
            for n in range(8):
                o = 16 * n
                mixed_a[:, n] = (keep_a[o : o + 16] + take_a[o : o + 16].astype(F32)).astype(BF16)
            for k in range(4):
                o = 128 + 16 * k
                v = (keep_a[o : o + 16] + take_a[o : o + 16].astype(F32)).astype(BF16)
                mixed_a[pl.ds(4 * chunk_of(k), 4), 8:12] = v.reshape(4, 4, 16, LANE)
            red_a[chip] = mixed_a[chip]

            def send(step, carry):
                to = (chip + step) % 16
                copy_to(mixed_a.at[to], red_a.at[chip], dir_s.at[4], dir_r.at[4], (s, 2 * to + c, r)).start()
                return carry

            lax.fori_loop(1, 16, send, 0)

        def emit(k):
            for i in range(nl):
                pt = block_of(2 + i, k)
                put_straight(pt, keep.at[k], give.at[k], 16 * i)
                put_turned(pt, keep.at[k], give.at[k], 16 * (nl + i))
            copy_to(
                give.at[k, 0 : 32 * nl], take.at[k, 0 : 32 * nl], pair_s.at[k], pair_r.at[k], at_core
            ).start()

        def spread(k):
            kk = chunk_of(k)
            wait_bytes(take.at[k, 0 : 32 * nl], pair_r.at[k])
            for b in range(nl):
                v = keep[k, 16 * b : 16 * b + 16] + take[k, 16 * b : 16 * b + 16].astype(F32)
                mixed_d[k, :, b] = v.astype(BF16)
                o = 16 * (nl + b)
                v = keep[k, o : o + 16] + take[k, o : o + 16].astype(F32)
                mixed_t[k, :, 4 * b : 4 * b + 4] = v.astype(BF16).reshape(4, 4, 16, LANE)
            red_d[k, chip, 0:nl] = mixed_d[k, chip, 0:nl]

            def send_direct(step, carry):
                to = (chip + step) % 16
                copy_to(
                    mixed_d.at[k, to, 0:nl],
                    red_d.at[k, chip, 0:nl],
                    dir_s.at[k],
                    dir_r.at[k],
                    (s, 2 * to + c, r),
                ).start()
                return carry

            lax.fori_loop(1, 16, send_direct, 0)

            def send_turned(step, carry):
                xd = (x + step) % 4
                copy_to(
                    mixed_t.at[k, xd, 0 : 4 * nl],
                    red_t.at[chip, 0 : 4 * nl],
                    tra_s.at[k],
                    tra_r.at[k],
                    (s, face_of(kk, xd, c), r),
                ).start()
                return carry

            lax.fori_loop(1, 4, send_turned, 0)
            if SHIFTS[k] == 0:
                red_t[chip, 0 : 4 * nl] = mixed_t[k, x, 0 : 4 * nl]
            else:
                send_turned(0, 0)

        def column_of(k, yi, odd):
            return (yi + (4 - SHIFTS[k] if odd else SHIFTS[k])) % 4

        def gather_early():
            wait_bytes(red_a.at[0:15], dir_r.at[4])
            for k in range(4):
                for yi in range(4):
                    for odd in range(2):
                        rows = slice(2 * k, 2 * k + 2)
                        part = red_a[4 * yi + odd, rows].astype(F32) + red_a[4 * yi + 2 + odd, rows].astype(F32)
                        j = column_of(k, yi, odd)
                        if k == 0 and odd == 0:
                            tot[j, 0:2] = part
                        else:
                            tot[j, 0:2] += part

        def gather_step(k):
            wait_bytes(red_d.at[0, 0:15, 0:nl], dir_r.at[k])
            for yi in range(4):
                for odd in range(2):
                    part = red_d[k, 4 * yi + odd, 0:nl].astype(F32) + red_d[k, 4 * yi + 2 + odd, 0:nl].astype(F32)
                    j = column_of(k, yi, odd)
                    if k == 0 and odd == 0:
                        tot[j, 2 : 2 + nl] = part
                    else:
                        tot[j, 2 : 2 + nl] += part

        def fold(b):
            for k in range(4):
                ls = slice(LANE * k, LANE * k + LANE)
                ln = slice(LANE * (k % 2), LANE * (k % 2) + LANE)
                rn = slice(8 * (k // 2), 8 * (k // 2) + 8)
                for q in range(2):
                    if b == 0:
                        piece_d[q, :, ls] = tot[k, 0, 8 * q : 8 * q + 8]
                    piece_n[q, b, rn, ln] = tot[k, 1 + b, 8 * q : 8 * q + 8]
            mixed_n[b] = piece_n[1 - r, b].astype(BF16)

        def fold_turned(b, total):
            for q in range(2):
                parts = [total[l, 8 * q : 8 * q + 8] for l in range(4)]
                top = jnp.concatenate(parts[0:2], axis=1)
                bottom = jnp.concatenate(parts[2:4], axis=1)
                piece_t[q, b] = jnp.concatenate([top, bottom], axis=0).astype(BF16)

        def add_early(i, acc):
            return acc + red_a[i, 8:12].astype(F32)

        def add_turned(i, acc):
            return acc + red_t[i, 0 : 4 * nl].astype(F32)

        def send_last(b):
            copies = [copy_to(mixed_n.at[b], fin_n.at[b], fin_s.at[7 + b], fin_r.at[9 + b], other_row)]
            if b == 0:
                copies.append(copy_to(piece_d.at[1 - r], fin_d, fin_s.at[0], fin_r.at[0], other_row))
            for q in range(2):
                copies.append(
                    copy_to(
                        piece_t.at[q, b],
                        fin_t.at[s, r],
                        fin_s.at[1 + 2 * b + q],
                        fin_r.at[1 + 2 * s + r],
                        (others_of[b], f, q),
                    )
                )
            for e in copies:
                e.start()
                ends.append(e)

        emit_early()
        if mid:
            wait_bytes(edge_end.at[0], edg_r.at[hfar])
            copy_to(edge_end.at[hfar], edge_far, edg_s.at[1], edg_r.at[3], at_mid).start()
        pass_end(3)
        pass_far(1)
        spread_early()
        late_product(0)
        late_product(1)
        pass_far(2)
        wait_bytes(edge_far, edg_r.at[3])
        if mid:
            copy_to(edge_far, edge_far, edg_s.at[3], edg_r.at[3], at_end).start()
            wait_bytes(edge_end.at[0], edg_r.at[hnear])
        emit(0)
        emit(1)
        spread(0)
        pass_far(3)
        spread(1)
        late_product(2)
        emit(2)
        late_product(3)
        emit(3)
        spread(2)
        spread(3)
        gather_early()
        ends = []
        others_of = [other_mid, other_end] + ([my_end] if mid else [])
        fold(0)
        fold_turned(0, lax.fori_loop(1, 16, add_early, red_a[0, 8:12].astype(F32)))
        send_last(0)
        lax.fori_loop(0, 22, put_column, 0)
        for k in range(4):
            gather_step(k)
        for k in range(4):
            wait_bytes(red_t.at[0 : (4 if SHIFTS[k] else 3), 0 : 4 * nl], tra_r.at[k])

        for b in range(1, nt):
            fold(b)
        rest_sum = lax.fori_loop(1, 16, add_turned, red_t[0, 0 : 4 * nl].astype(F32))
        for b in range(1, nt):
            fold_turned(b, rest_sum[4 * b - 4 : 4 * b])
            send_last(b)
        wait_bytes(fin_d, fin_r.at[0])
        for b in range(nt):
            wait_bytes(fin_n.at[b], fin_r.at[9 + b])
        sources = [other_mid, other_end] + ([] if mid else [my_mid])
        for p in sources:
            for q in range(2):
                wait_bytes(fin_t.at[p, q], fin_r.at[1 + 2 * p + q])

        def put(block, value):
            gram[:, pl.ds(pl.multiple_of(block * BLK, BLK), BLK)] = value * GRAM_SCALE

        def put_folded(block, value):
            put(block, jnp.concatenate([value[0:8], value[8:16]], axis=1))

        def turned(p):
            return fin_t[p, 0].astype(F32) + fin_t[p, 1].astype(F32)

        def straight(b):
            return piece_n[r, b] + fin_n[b].astype(F32)

        put(s, piece_d[r] + fin_d[...])
        put_folded(other_mid, straight(0) + turned(other_mid))
        put_folded(other_end, straight(1) + turned(other_end))
        if mid:
            put_folded(my_end, straight(2))
        else:
            put_folded(my_mid, turned(my_mid))

        for e in ends:
            e.wait_send()
        for k in range(4):
            wait_bytes(own.at[0, 0], str_s.at[0, k])
            wait_bytes(own.at[0, 0], str_s.at[1, k])
            if mid:
                wait_bytes(own.at[0, 0], str_s.at[2, k])
                wait_bytes(own.at[0, 0], str_s.at[3, k])
            wait_bytes(edge_own.at[0], edg_s.at[k]) if mid or k < 2 else None
            wait_bytes(give.at[k, 0 : 32 * nl], pair_s.at[k])
            wait_bytes(mixed_d.at[0, 0:15, 0:nl], dir_s.at[k])
            wait_bytes(red_t.at[0 : (4 if SHIFTS[k] else 3), 0 : 4 * nl], tra_s.at[k])
        wait_bytes(give_a, pair_s.at[4])
        wait_bytes(mixed_a.at[0:15], dir_s.at[4])

    @on_mid
    def _():
        plane(True)

    @on_end
    def _():
        plane(False)

    za.wait_send()
    zb.wait_send()
    for p in range(2):
        for step in range(1, 4):
            wait_bytes(lines.at[p], halo_s.at[1 + 3 * p + step])
            wait_bytes(arrived.at[0, 0, 0], halo_s.at[9 + 3 * p + step])

            @pl.when(r == 1)
            def _():
                wait_bytes(arrived.at[0, 0, 0], halo_s.at[15 + 3 * p + step])

        wait_bytes(gathered.at[p, 0], halo_s.at[8 + p])


def per_device(surface_field, ocean_mask, cell_area, tile_links, edge_turns):
    vmem = pl.BlockSpec(memory_space=pltpu.VMEM)
    smem = pl.BlockSpec(memory_space=pltpu.SMEM)
    dma = pltpu.SemaphoreType.DMA
    links = jnp.concatenate([tile_links.T, edge_turns.T], axis=0)
    return pl.pallas_call(
        kernel,
        out_shape=(
            jax.ShapeDtypeStruct((1, ROWS, SIDE, BLK), BF16),
            jax.ShapeDtypeStruct((8, SNAPS), F32),
        ),
        in_specs=[smem, vmem, vmem, vmem],
        out_specs=(vmem, vmem),
        scratch_shapes=[
            pltpu.VMEM((32, BLK), F32),
            pltpu.VMEM((ROWS, BLK), F32),
            pltpu.VMEM((32, BLK), BF16),
            pltpu.VMEM((32, BLK), BF16),
            pltpu.VMEM((SIDE, BLK), BF16),
            pltpu.VMEM((2, 2, SIDE, 256), BF16),
            pltpu.VMEM((2, 2, 4, 2, SIDE, 256), BF16),
            pltpu.VMEM((2, 4, 2, SIDE, 256), BF16),
            pltpu.VMEM((2, 4, 2, SIDE, 256), BF16),
            pltpu.VMEM((32, BLK), F32),
            pltpu.VMEM((SIDE, BLK), F32),
            pltpu.VMEM((ROWS, SIDE, BLK), F32),
            pltpu.VMEM((ROWS, BLK), F32),
            pltpu.VMEM((2, 64, BLK), F32),
            pltpu.VMEM((4, SIDE, LANE), F32),
            pltpu.VMEM((4, SIDE, LANE), F32),
            pltpu.VMEM((3, 22, SIDE, LANE), BF16),
            pltpu.VMEM((3, 2, 64, LANE), F32),
            pltpu.VMEM((3, LANE, BLK), F32),
            pltpu.VMEM((4, 2, 11, SIDE, LANE), BF16),
            pltpu.VMEM((4, 2, 11, SIDE, LANE), BF16),
            pltpu.VMEM((4, 11, SIDE, LANE), BF16),
            pltpu.VMEM((4, 11, SIDE, LANE), BF16),
            pltpu.VMEM((2, 64, BLK), BF16),
            pltpu.VMEM((2, 4, 64, LANE), BF16),
            pltpu.VMEM((2, 4, 64, LANE), BF16),
            pltpu.VMEM((4, 64, LANE), BF16),
            pltpu.VMEM((4, 64, LANE), BF16),
            pltpu.VMEM((4, 4, LANE, BLK), F32),
            pltpu.VMEM((192, 16, LANE), F32),
            pltpu.VMEM((192, 16, LANE), BF16),
            pltpu.VMEM((192, 16, LANE), BF16),
            pltpu.VMEM((16, 12, 16, LANE), BF16),
            pltpu.VMEM((16, 12, 16, LANE), BF16),
            pltpu.VMEM((4, 64, 16, LANE), F32),
            pltpu.VMEM((4, 64, 16, LANE), BF16),
            pltpu.VMEM((4, 64, 16, LANE), BF16),
            pltpu.VMEM((4, 16, 2, 16, LANE), BF16),
            pltpu.VMEM((4, 4, 8, 16, LANE), BF16),
            pltpu.VMEM((4, 16, 2, 16, LANE), BF16),
            pltpu.VMEM((16, 8, 16, LANE), BF16),
            pltpu.VMEM((4, 4, 16, LANE), F32),
            pltpu.VMEM((2, 8, BLK), F32),
            pltpu.VMEM((2, 3, 16, 256), F32),
            pltpu.VMEM((2, 3, 16, 256), BF16),
            pltpu.VMEM((3, 16, 256), BF16),
            pltpu.VMEM((8, BLK), F32),
            pltpu.VMEM((3, 16, 256), BF16),
            pltpu.VMEM((4, 2, 16, 256), BF16),
            dma((22,)),
            dma((22,)),
            dma((2, 4)),
            dma((2, 4)),
            dma((4, 4)),
            dma((4, 2)),
            dma((4,)),
            dma((4,)),
            dma((4,)),
            dma((4,)),
            dma((5,)),
            dma((5,)),
            dma((5,)),
            dma((5,)),
            dma((4,)),
            dma((4,)),
            dma((10,)),
            dma((12,)),
        ],
        compiler_params=pltpu.CompilerParams(
            collective_id=0, has_side_effects=True, vmem_limit_bytes=56 * 1024 * 1024
        ),
        name="slope_gram",
    )(links, surface_field, ocean_mask, cell_area)


def solution(mesh):
    placed = (
        P("face", "row", None, "snapshot"),
        P("face", "row", None),
        P("face", "row", None),
        P(),
        P(),
    )
    return jax.shard_map(
        per_device,
        mesh=mesh,
        in_specs=placed,
        out_specs=(P("face", "row", None, "snapshot"), P(("snapshot", "face", "row"), None)),
        check_vma=False,
    )
```
